128 devices in a mesh: feat: 4 (over y), vert: 32 (over x, z, core).
Axes of the slice: x: 4, y: 4, z: 4, core: 2. Of those that a mesh axis runs over, the one named last changes fastest.
Arguments:
- features: bfloat16 [12288, 768], P('vert', 'feat'), may hold values from -18 to 18
- counts: int32 [12288, 12288], P('vert'), may hold values from 0 to 3, as said below
- tile_mask: int32 [96, 96], P('vert'), may hold values 0 or 1
- w_in: bfloat16 [768, 1024], P('feat'), may hold values from -0.21875 to 0.21875
- b_in: float32 [1024], P('feat'), may hold values from -3 to 3
- w_out: bfloat16 [1024, 153], P('feat'), may hold values from -0.5625 to 0.5625
- b_out: float32 [153], replicated, may hold values from -6 to 6
Outputs:
- logits: float32 [12288, 153], P('vert')
The draws below stay inside these ranges and needn't reach their ends.
Inputs may be any that keep to these rules, and one draw needn't show every extreme that they name: Entry (i, j) counts edges from vertex j to vertex i; only entries inside tiles whose tile_mask entry is 1 are edges. `tile_mask`: 1 marks a stored tile of 128 x 128 entries of counts.
All inputs are finite; a program needn't handle non-finite values. No bound on the sum of `tile_mask` on one device may be relied on, other than what follows from the above.
Results may differ from the reference program's by a relative error of at most 0.007.
Values may be sent and summed in bfloat16 or wider, within the bound.
No kernel may reach another device: no remote copies, remote signals or barrier semaphores. Data moves between devices by JAX's collectives and lax.ppermute only.
A program may use at most 128 MiB of HBM per device.

```python
import jax
import jax.numpy as jnp
from jax import lax

F_IN = 768
HID = 1024
CLS = 153
TILE = 128
V_DEV = 384
V = 12288
N_VERT = 32


def draw_counts(key, part):
    key = jax.random.fold_in(key, 11)
    first_key, second_key = jax.random.split(key)
    chance = jax.random.randint(first_key, (V, V), 0, V)
    multiple = jax.random.randint(second_key, (V, V), 1, 4)
    return jnp.where(chance < 32, multiple, 0).astype(jnp.int32)


def plant(result, key, low, high):
    extent = result.shape
    spot = [jax.random.randint(jax.random.fold_in(key, axis), (), 0, extent[axis]) for axis in range(len(extent))]
    result = result.at[tuple(spot)].set(low)
    longest = extent.index(max(extent))
    spot[longest] = (spot[longest] + 1) % extent[longest]
    return result.at[tuple(spot)].set(high)


def levels(own_key, dims, cuts, least, largest):
    factor_of = 1.0
    for position, parts in cuts:
        heights = jax.random.uniform(jax.random.fold_in(jax.random.fold_in(own_key, 6), position), (parts,), jnp.float32, least / len(cuts), largest / len(cuts))
        factor_of = factor_of * jnp.repeat(jnp.exp(heights), dims[position] // parts).reshape((-1,) + (1,) * (len(dims) - 1 - position))
    return factor_of


def normal_values(own_key, dims, width, limit, shards=(), held_as=jnp.bfloat16):
    entries = width * jax.random.normal(own_key, dims, jnp.float32)
    if shards:
        entries = entries * levels(own_key, dims, shards, -0.22, 0.18)
    return jnp.clip(entries, -limit, limit).astype(held_as)


def setup_inputs(seed: int = 0) -> dict:
    arg_keys = jax.random.split(jax.random.key(seed), 8)
    return {
        "features": normal_values(arg_keys[0], (V, F_IN), 3.0, 18.0, ((0, 32), (1, 4))),
        "counts": draw_counts(jax.random.fold_in(arg_keys[7], 71), 0),
        "tile_mask": plant((jax.random.randint(arg_keys[2], (V // TILE, V // TILE), 0, 4) < 1).astype(jnp.int32), jax.random.fold_in(arg_keys[2], 1), 0, 1),
        "w_in": normal_values(arg_keys[3], (F_IN, HID), F_IN ** -0.5, 0.21875, ((0, 4),)),
        "b_in": normal_values(arg_keys[4], (HID,), 0.5, 3.0, ((0, 4),), jnp.float32),
        "w_out": normal_values(arg_keys[5], (HID, CLS), (3.0 * HID ** -0.5), 0.5625, ((0, 4),)),
        "b_out": normal_values(arg_keys[6], (CLS,), 1.0, 6.0, (), jnp.float32),
    }


def adjacency(count_rows, mask_rows, first_row):
    spread = jnp.repeat(jnp.repeat(mask_rows, TILE, axis=0), TILE, axis=1)
    shape = count_rows.shape
    columns = lax.broadcasted_iota(jnp.int32, shape, 1)
    diagonal = lax.broadcasted_iota(jnp.int32, shape, 0) + first_row
    return count_rows * spread + (columns == diagonal).astype(jnp.int32)


def reference(features, counts, tile_mask, w_in, b_in, w_out, b_out):
    feats = features.astype(jnp.float32)
    w_first = w_in.astype(jnp.float32)
    w_second = w_out.astype(jnp.float32)
    tiles_dev = V_DEV // TILE

    def block_adjacency(block):
        first = (block * V_DEV).astype(jnp.int32)
        count_rows = lax.dynamic_slice_in_dim(counts, first, V_DEV, 0)
        mask_rows = lax.dynamic_slice_in_dim(tile_mask, (block * tiles_dev).astype(jnp.int32), tiles_dev, 0)
        adj = adjacency(count_rows, mask_rows, first).astype(jnp.float32)
        degree = jnp.sum(adj, axis=1, keepdims=True)
        return adj, degree

    def layer_one(block):
        adj, degree = block_adjacency(block)
        mean = jnp.dot(adj, feats, precision=lax.Precision.HIGHEST) / degree
        pre = jnp.dot(mean, w_first, precision=lax.Precision.HIGHEST) + b_in
        return jnp.maximum(pre, 0.0).astype(jnp.bfloat16)

    blocks = jnp.arange(N_VERT, dtype=jnp.int32)
    hidden = lax.map(layer_one, blocks).reshape(V, HID).astype(jnp.float32)

    def layer_two(block):
        adj, degree = block_adjacency(block)
        mean = jnp.dot(adj, hidden, precision=lax.Precision.HIGHEST) / degree
        return jnp.dot(mean, w_second, precision=lax.Precision.HIGHEST) + b_out

    return lax.map(layer_two, blocks).reshape(V, CLS)
```

```python
import jax
import jax.numpy as jnp
from jax import lax
from jax.experimental import pallas as pl
from jax.experimental.pallas import tpu as pltpu
from jax.sharding import PartitionSpec as P

TILE = 128
ROWS = 384
NV = 32
NF = 4
SHARE = ROWS // NF
CLS = 153
bf16 = jnp.bfloat16
f32 = jnp.float32
NT = (((1,), (1,)), ((), ()))
VM = pl.BlockSpec(memory_space=pltpu.VMEM)
SM = pl.BlockSpec(memory_space=pltpu.SMEM)


def params(mib=16):
    return pltpu.CompilerParams(vmem_limit_bytes=mib * 2**20)


def cost(flops, nbytes):
    return pl.CostEstimate(flops=int(flops), bytes_accessed=int(nbytes), transcendentals=0)


def positions(move):
    pairs = []
    for x in range(4):
        for z in range(4):
            for c in range(2):
                xx, zz, cc = move(x, z, c)
                pairs.append(((x * 4 + z) * 2 + c, (xx % 4 * 4 + zz % 4) * 2 + cc % 2))
    return pairs


def first_axis(value, shift):
    return lax.ppermute(value, "vert", positions(lambda x, z, c: (x + shift * (1 - c), z + shift * c, c)))


def second_axis(value, shift):
    return lax.ppermute(value, "vert", positions(lambda x, z, c: (x + shift * c, z + shift * (1 - c), c)))


def swap(value):
    return lax.ppermute(value, "vert", positions(lambda x, z, c: (x, z, 1 - c)))


def along_feat(value, shift):
    return lax.ppermute(value, "feat", [(i, (i + shift) % NF) for i in range(NF)])


CHUNK = 2 * ROWS


def adjacency_kernel(mask, where, counts, adj, adj2, degree):
    step = pl.program_id(0)
    me, feat = where[0], where[1]
    row = lax.broadcasted_iota(jnp.int32, (TILE, TILE), 0)
    col = lax.broadcasted_iota(jnp.int32, (TILE, TILE), 1)
    eye = (row == col).astype(f32)

    @pl.when(step == 0)
    def _():
        degree[...] = jnp.zeros_like(degree)

    for i in range(ROWS // TILE):
        total = degree[i * TILE : (i + 1) * TILE, :]
        for j in range(CHUNK // TILE):
            tile_col = step * (CHUNK // TILE) + j
            stored = mask[i, tile_col].astype(f32)
            own = (me * (ROWS // TILE) + i == tile_col).astype(f32)
            tile = counts[i * TILE : (i + 1) * TILE, j * TILE : (j + 1) * TILE].astype(f32)
            tile = tile * stored + eye * own
            total = total + tile
            adj[i * TILE : (i + 1) * TILE, j * TILE : (j + 1) * TILE] = tile.astype(bf16)
        degree[i * TILE : (i + 1) * TILE, :] = total

    source = lax.broadcasted_iota(jnp.int32, (ROWS, TILE), 0)
    target = lax.broadcasted_iota(jnp.int32, (ROWS, TILE), 1)
    pick = ((source == target + feat * SHARE) & (target < SHARE)).astype(f32).astype(bf16)
    for j in range(CHUNK // ROWS):
        part = jnp.dot(adj[:, j * ROWS : (j + 1) * ROWS], pick, preferred_element_type=f32)
        adj2[:, j * TILE : (j + 1) * TILE] = part.astype(bf16)

    @pl.when(step == pl.num_programs(0) - 1)
    def _():
        degree[...] = jnp.broadcast_to(jnp.sum(degree[...], axis=1, keepdims=True), degree.shape)


def make_adjacency(tile_mask, where, counts):
    n = NV * ROWS // CHUNK
    return pl.pallas_call(
        adjacency_kernel,
        grid_spec=pltpu.PrefetchScalarGridSpec(
            num_scalar_prefetch=2,
            grid=(n,),
            in_specs=[pl.BlockSpec((ROWS, CHUNK), lambda i, *_: (0, i))],
            out_specs=[
                pl.BlockSpec((ROWS, CHUNK), lambda i, *_: (0, i)),
                pl.BlockSpec((ROWS, CHUNK // ROWS * TILE), lambda i, *_: (0, i)),
                pl.BlockSpec((ROWS, TILE), lambda i, *_: (0, 0)),
            ],
        ),
        out_shape=[
            jax.ShapeDtypeStruct((ROWS, NV * ROWS), bf16),
            jax.ShapeDtypeStruct((ROWS, NV * TILE), bf16),
            jax.ShapeDtypeStruct((ROWS, TILE), f32),
        ],
        compiler_params=params(),
        cost_estimate=cost(2.4e9, 31e6),
        name="adjacency",
    )(tile_mask, where, counts)


def add_blocks(order, adj, total, pieces):
    k = 0
    for piece in pieces:
        for b in range(piece.shape[0]):
            src = pl.multiple_of(order[k] * ROWS, ROWS)
            total = total + lax.dot_general(adj[:, pl.ds(src, ROWS)], piece[b], NT, preferred_element_type=f32)
            k += 1
    return total


def product_first(order, adj, *refs):
    refs[-1][...] = add_blocks(order, adj, jnp.zeros(refs[-1].shape, f32), refs[:-1])


def product_next(order, adj, before, *refs):
    refs[-1][...] = add_blocks(order, adj, before[...], refs[:-1])


def product_last(order, where, adj, before, degree, *refs):
    pieces, outs, mean = refs[:-5], refs[-5:-1], refs[-1]
    total = add_blocks(order, adj, before[...], pieces)
    mean[...] = total / degree[:, :1]
    for s in range(NF):
        q = (where[1] + s) % NF
        outs[s][...] = mean[pl.ds(pl.multiple_of(q * SHARE, SHARE), SHARE), :].astype(bf16)


def blocks_cost(pieces):
    n = sum(p.shape[0] for p in pieces)
    return cost(2 * 384 * 384 * 256 * n, n * 450e3)


def hidden_kernel(where, g0, g1, g2, g3, own, near, far, z_out, hid):
    feat, core = where[1], where[2]
    gs = (g0, g1, g2, g3)
    total = jnp.zeros((SHARE, 256), f32)
    for h in range(2):
        half = (core + h) % 2
        def part(s, rows, h=h, half=half):
            if s == 0:
                return own[half, rows, :]
            return (near, far)[h][s - 1, rows, :]
        pre = jnp.zeros((SHARE, 512), f32)
        for s in range(NF):
            pre = pre + jnp.dot(gs[s][...], part(s, slice(0, 192)), preferred_element_type=f32)
        hid[...] = pre
        for s in range(NF):
            owner = (feat + NF - s) % NF
            lanes = pl.ds(pl.multiple_of(owner * TILE, TILE), TILE)
            b = part(s, slice(256, 272))[:, :TILE].astype(f32)
            bias = b[0:1] + b[1:2] + b[2:3]
            unit = jnp.maximum(hid[:, lanes] + bias, 0.0).astype(bf16)
            w = part(s, slice(192, 256))
            total = total + jnp.dot(unit[:, :64], w[:, :256], preferred_element_type=f32)
            total = total + jnp.dot(unit[:, 64:], w[:, 256:], preferred_element_type=f32)
    z_out[0:SHARE, :] = total[:, :TILE].astype(bf16)
    tail = total[:, TILE : TILE + 32]
    packed = jnp.concatenate([tail[0:32], tail[32:64], tail[64:96], jnp.zeros((32, 32), f32)], axis=1)
    z_out[SHARE:, :] = packed.astype(bf16)


def scores_kernel(order, adj2, degree, z_near, z_far, out, z_all):
    k = 0
    for piece in (z_near, z_far):
        for b in range(piece.shape[0]):
            src = pl.multiple_of(order[k] * TILE, TILE)
            z_all[pl.ds(src, TILE), :TILE] = piece[b]
            tail = piece[b, SHARE:, :].astype(f32)
            tail = jnp.concatenate([tail[:, 0:32], tail[:, 32:64], tail[:, 64:96], jnp.zeros((32, 32), f32)], axis=0)
            tail = jnp.concatenate([tail, jnp.zeros((TILE, 96), f32)], axis=1)
            z_all[pl.ds(src, TILE), TILE:] = tail.astype(bf16)
            k += 1
    part = jnp.dot(adj2[...], z_all[...], preferred_element_type=f32) / degree[:, :1]
    out[0:ROWS, :] = part[:, :TILE].astype(bf16)
    tail = part[:, TILE : TILE + 32]
    packed = jnp.concatenate([tail[i * SHARE : (i + 1) * SHARE] for i in range(NF)], axis=1)
    out[ROWS:, :] = packed.astype(bf16)


def sum_kernel(p0, p1, p2, p3, b_out, out):
    total = (p0[...].astype(f32) + p2[...].astype(f32)) + (p1[...].astype(f32) + p3[...].astype(f32))
    out[:, :TILE] = total[:ROWS] + b_out[:, :TILE]
    for i in range(NF):
        out[i * SHARE : (i + 1) * SHARE, TILE:] = (
            total[ROWS:, i * 32 : i * 32 + CLS - TILE] + b_out[:, TILE:]
        )


def local(features, counts, tile_mask, w_in, b_in, w_out, b_out):
    me = lax.axis_index("vert").astype(jnp.int32)
    feat = lax.axis_index("feat").astype(jnp.int32)
    core, spot = me % 2, me // 2
    x, z = spot // 4, spot % 4
    where = jnp.stack([me, feat, core])

    def source(s, t, c):
        first, second = jnp.where(c == 0, x, z), jnp.where(c == 0, z, x)
        first, second = (first + NF - s) % NF, (second + NF - t) % NF
        xx, zz = jnp.where(c == 0, first, second), jnp.where(c == 0, second, first)
        return (xx * 4 + zz) * 2 + c

    order = jnp.stack([source(s, t, c) for t in (0, 1, 3, 2) for c in (core, 1 - core) for s in (0, 1, 3, 2)])

    mine = features.T
    ring = [first_axis(mine, s) for s in (1, 3, 2)]
    four = jnp.stack([mine] + ring)
    rows = {t: second_axis(four, t) for t in (1, 3, 2)}

    tail = jnp.pad(w_out, ((0, 0), (0, 256 - CLS))).reshape(2, 2, 64, 256).transpose(0, 2, 1, 3).reshape(2, 64, 512)
    hi = lax.reduce_precision(b_in, 8, 7)
    mid = lax.reduce_precision(b_in - hi, 8, 7)
    low = b_in - hi - mid
    bias = jnp.stack([hi, mid, low]).astype(bf16).reshape(3, 2, TILE).transpose(1, 0, 2)
    bias = jnp.pad(bias, ((0, 0), (0, 13), (0, 512 - TILE)))
    halves = w_in.reshape(192, 4, 2, TILE).transpose(2, 0, 1, 3).reshape(2, 192, 512)
    own = jnp.concatenate([halves, tail, bias], axis=1)
    half = lax.dynamic_index_in_dim(own, core, 0, keepdims=False)
    near = jnp.stack([along_feat(half, s) for s in (1, 2, 3)])
    far = swap(near)

    adj, adj2, degree = make_adjacency(tile_mask, where, counts)

    total_shape = jax.ShapeDtypeStruct((ROWS, 192), f32)
    pieces = [four, swap(four)]
    total = pl.pallas_call(
        product_first, out_shape=total_shape, in_specs=[SM] + [VM] * 3, out_specs=VM,
        compiler_params=params(), cost_estimate=blocks_cost(pieces), name="product_first",
    )(order[0:8], adj, *pieces)
    pieces = [rows[1], swap(rows[1]), rows[3], swap(rows[3])]
    total = pl.pallas_call(
        product_next, out_shape=total_shape, in_specs=[SM] + [VM] * 6, out_specs=VM,
        compiler_params=params(), cost_estimate=blocks_cost(pieces), name="product_next",
    )(order[8:24], adj, total, *pieces)
    pieces = [rows[2], swap(rows[2])]
    means = pl.pallas_call(
        product_last, out_shape=[jax.ShapeDtypeStruct((SHARE, 192), bf16)] * NF,
        in_specs=[SM] * 2 + [VM] * 5, out_specs=[VM] * NF,
        scratch_shapes=[pltpu.VMEM((ROWS, 192), f32)],
        compiler_params=params(), cost_estimate=blocks_cost(pieces), name="product_last",
    )(order[24:32], where, adj, total, degree, *pieces)

    g = [means[0]] + [along_feat(means[s], s) for s in (1, 2, 3)]
    z_block = pl.pallas_call(
        hidden_kernel, out_shape=jax.ShapeDtypeStruct((TILE, TILE), bf16),
        in_specs=[SM] + [VM] * 7, out_specs=VM,
        scratch_shapes=[pltpu.VMEM((SHARE, 512), f32)],
        compiler_params=params(), cost_estimate=cost(2 * 96 * 768 * 1024, 2e6), name="hidden",
    )(where, *g, own, near, far)

    z_four = jnp.stack([z_block] + [first_axis(z_block, s) for s in (1, 3, 2)])
    z_near = jnp.concatenate([z_four] + [second_axis(z_four, t) for t in (1, 3, 2)])
    z_far = swap(z_near)
    order2 = jnp.stack([source(s, t, c) for c in (core, 1 - core) for t in (0, 1, 3, 2) for s in (0, 1, 3, 2)])
    part = pl.pallas_call(
        scores_kernel, out_shape=jax.ShapeDtypeStruct((ROWS + SHARE, TILE), bf16),
        in_specs=[SM] + [VM] * 4, out_specs=VM,
        scratch_shapes=[pltpu.VMEM((NV * TILE, 256), bf16)],
        compiler_params=params(), cost_estimate=cost(2 * 384 * 4096 * 256, 5e6), name="scores",
    )(order2, adj2, degree, z_near, z_far)
    parts = [part] + [along_feat(part, s) for s in (1, 2, 3)]
    return pl.pallas_call(
        sum_kernel, out_shape=jax.ShapeDtypeStruct((ROWS, CLS), f32),
        in_specs=[VM] * 5, out_specs=VM,
        compiler_params=params(), cost_estimate=cost(3e5, 8e5), name="sum",
    )(*parts, b_out.reshape(1, CLS))


def solution(mesh):
    placed = (
        P("vert", "feat"),
        P("vert", None),
        P("vert", None),
        P("feat", None),
        P("feat"),
        P("feat", None),
        P(),
    )
    return jax.shard_map(
        local, mesh=mesh, in_specs=placed, out_specs=P("vert", None), check_vma=False
    )
```

```python
import jax
import jax.numpy as jnp
from jax import lax
from jax.experimental import pallas as pl
from jax.experimental.pallas import tpu as pltpu
from jax.sharding import PartitionSpec as P

TILE = 128
ROWS = 384
NV = 32
NF = 4
SHARE = ROWS // NF
CLS = 153
bf16 = jnp.bfloat16
f32 = jnp.float32
NT = (((1,), (1,)), ((), ()))
VM = pl.BlockSpec(memory_space=pltpu.VMEM)
SM = pl.BlockSpec(memory_space=pltpu.SMEM)


def here():
    return lax.axis_index("vert").astype(jnp.int32), lax.axis_index("feat").astype(jnp.int32)


def source(me, s, t, c):
    spot = lax.div(me, 2)
    x, z = lax.div(spot, NF), lax.rem(spot, NF)
    x = lax.rem(x + NF - jnp.where(c == 0, s, t), NF)
    z = lax.rem(z + NF - jnp.where(c == 0, t, s), NF)
    return (x * NF + z) * 2 + c


SHIFTS = (0, 1, 3, 2)


def params(mib=16):
    return pltpu.CompilerParams(vmem_limit_bytes=mib * 2**20)


def cost(flops, nbytes):
    return pl.CostEstimate(flops=int(flops), bytes_accessed=int(nbytes), transcendentals=0)


def positions(move):
    pairs = []
    for x in range(4):
        for z in range(4):
            for c in range(2):
                xx, zz, cc = move(x, z, c)
                pairs.append(((x * 4 + z) * 2 + c, (xx % 4 * 4 + zz % 4) * 2 + cc % 2))
    return pairs


def first_axis(value, shift):
    return lax.ppermute(value, "vert", positions(lambda x, z, c: (x + shift * (1 - c), z + shift * c, c)))


def second_axis(value, shift):
    return lax.ppermute(value, "vert", positions(lambda x, z, c: (x + shift * c, z + shift * (1 - c), c)))


def swap(value):
    return lax.ppermute(value, "vert", positions(lambda x, z, c: (x, z, 1 - c)))


def along_feat(value, shift):
    return lax.ppermute(value, "feat", [(i, (i + shift) % NF) for i in range(NF)])


CHUNK = 2 * ROWS
STEPS = NV * ROWS // CHUNK
SLOTS = 4


def adjacency_kernel(mask, counts, adj, adj2, degree, slots, sems):
    me, feat = here()
    row = lax.broadcasted_iota(jnp.int32, (TILE, TILE), 0)
    col = lax.broadcasted_iota(jnp.int32, (TILE, TILE), 1)
    eye = (row == col).astype(f32)
    source = lax.broadcasted_iota(jnp.int32, (ROWS, TILE), 0)
    target = lax.broadcasted_iota(jnp.int32, (ROWS, TILE), 1)
    pick = ((source == target + feat * SHARE) & (target < SHARE)).astype(f32).astype(bf16)

    def fetch(step, slot):
        start = pl.multiple_of(step * CHUNK, CHUNK)
        return pltpu.make_async_copy(counts.at[:, pl.ds(start, CHUNK)], slots.at[slot], sems.at[slot])

    for i in range(SLOTS - 1):
        fetch(i, i).start()
    degree[...] = jnp.zeros_like(degree)

    @pl.loop(0, STEPS)
    def _(step):
        slot = lax.rem(step, SLOTS)

        @pl.when(step + SLOTS - 1 < STEPS)
        def _():
            fetch(step + SLOTS - 1, lax.rem(step + SLOTS - 1, SLOTS)).start()

        fetch(step, slot).wait()
        for j in range(CHUNK // ROWS):
            base = pl.multiple_of(step * CHUNK + j * ROWS, ROWS)
            for k in range(ROWS // TILE):
                tile_col = step * (CHUNK // TILE) + j * (ROWS // TILE) + k
                for i in range(ROWS // TILE):
                    stored = mask[i, tile_col].astype(f32)
                    own = (me * (ROWS // TILE) + i == tile_col).astype(f32)
                    tile = slots[slot, i * TILE : (i + 1) * TILE, j * ROWS + k * TILE : j * ROWS + (k + 1) * TILE]
                    tile = tile.astype(f32) * stored + eye * own
                    degree[i * TILE : (i + 1) * TILE, :] += tile
                    adj[i * TILE : (i + 1) * TILE, pl.ds(base + k * TILE, TILE)] = tile.astype(bf16)
            part = jnp.dot(adj[:, pl.ds(base, ROWS)], pick, preferred_element_type=f32)
            place = pl.multiple_of((step * (CHUNK // ROWS) + j) * TILE, TILE)
            adj2[:, pl.ds(place, TILE)] = part.astype(bf16)

    degree[...] = jnp.broadcast_to(jnp.sum(degree[...], axis=1, keepdims=True), degree.shape)


def make_adjacency(tile_mask, counts):
    counts = pltpu.with_memory_space_constraint(counts, pltpu.HBM)
    return pl.pallas_call(
        adjacency_kernel,
        in_specs=[SM, pl.BlockSpec(memory_space=pltpu.HBM)],
        out_specs=[VM] * 3,
        out_shape=[
            pltpu.VMEM((ROWS, NV * ROWS), bf16),
            pltpu.VMEM((ROWS, NV * TILE), bf16),
            pltpu.VMEM((ROWS, TILE), f32),
        ],
        scratch_shapes=[pltpu.VMEM((SLOTS, ROWS, CHUNK), jnp.int32), pltpu.SemaphoreType.DMA((SLOTS,))],
        compiler_params=params(),
        cost_estimate=cost(2.4e9, 31e6),
        name="adjacency",
    )(tile_mask, counts)


def pack_kernel(w_in, w_out_t, b_in, after, mine, other):
    core = lax.rem(here()[0], 2)
    zero = jnp.zeros((192 - CLS, TILE), f32)
    for out, half in ((mine, core), (other, 1 - core)):
        for k in range(NF):
            lanes = pl.ds(pl.multiple_of(256 * k + TILE * half, TILE), TILE)
            out[0:192, k * TILE : (k + 1) * TILE] = w_in[:, lanes]
        lanes = pl.ds(pl.multiple_of(TILE * half, TILE), TILE)
        w = jnp.concatenate([w_out_t[:, lanes].astype(f32), zero], axis=0)
        for k in range(NF):
            out[192:240, k * TILE : (k + 1) * TILE] = w[48 * k : 48 * (k + 1)].astype(bf16)
        b = jnp.broadcast_to(b_in[:, lanes], (16, TILE))
        hi = b.astype(bf16).astype(f32)
        mid = (b - hi).astype(bf16).astype(f32)
        low = b - hi - mid
        row = lax.broadcasted_iota(jnp.int32, (16, TILE), 0)
        b = jnp.where(row == 0, hi, jnp.where(row == 1, mid, jnp.where(row == 2, low, 0.0)))
        out[240:256, 0:TILE] = b.astype(bf16)
        out[240:256, TILE:] = jnp.zeros((16, 512 - TILE), bf16)


def stack_kernel(a, b, c, d, after, out):
    for i, part in enumerate((a, b, c, d)):
        out[i] = part[...]


def add_blocks(shifts, adj, total, pieces):
    me, _ = here()
    for p, piece in enumerate(pieces):
        core = lax.rem(me + p, 2)
        for b in range(NF):
            src = source(me, SHIFTS[b], shifts[p // 2], core)
            src = pl.multiple_of(src * ROWS, ROWS)
            total = total + lax.dot_general(adj[:, pl.ds(src, ROWS)], piece[b], NT, preferred_element_type=f32)
    return total


def product_first(adj, *refs):
    refs[-1][...] = add_blocks((0,), adj, jnp.zeros(refs[-1].shape, f32), refs[:-1])


def product_next(adj, before, *refs):
    refs[-1][...] = add_blocks((1, 3), adj, before[...], refs[:-1])


def product_last(adj, before, degree, *refs):
    pieces, outs, mean = refs[:-5], refs[-5:-1], refs[-1]
    feat = here()[1]
    total = add_blocks((2,), adj, before[...], pieces)
    mean[...] = total / degree[:, :1]
    for s in range(NF):
        q = lax.rem(feat + s, NF)
        outs[s][...] = mean[pl.ds(pl.multiple_of(q * SHARE, SHARE), SHARE), :].astype(bf16)


def blocks_cost(pieces):
    n = sum(p.shape[0] for p in pieces)
    return cost(2 * 384 * 384 * 256 * n, n * 450e3)


def hidden_kernel(g0, g1, g2, g3, n0, n1, n2, n3, f0, f1, f2, f3, z_out, hid):
    feat = here()[1]
    gs = (g0, g1, g2, g3)
    total = jnp.zeros((SHARE, 192), f32)
    for parts in ((n0, n1, n2, n3), (f0, f1, f2, f3)):
        pre = jnp.zeros((SHARE, 512), f32)
        for s in range(NF):
            pre = pre + jnp.dot(gs[s][...], parts[s][0:192, :], preferred_element_type=f32)
        hid[...] = pre
        for s in range(NF):
            owner = lax.rem(feat + NF - s, NF)
            lanes = pl.ds(pl.multiple_of(owner * TILE, TILE), TILE)
            b = parts[s][240:256, 0:TILE].astype(f32)
            bias = b[0:1] + b[1:2] + b[2:3]
            unit = jnp.maximum(hid[:, lanes] + bias, 0.0).astype(bf16)
            w = parts[s][192:240, :]
            w = jnp.concatenate([w[:, k * TILE : (k + 1) * TILE] for k in range(NF)], axis=0)
            total = total + lax.dot_general(unit, w, NT, preferred_element_type=f32)
    z_out[0:SHARE, :] = total[:, :TILE].astype(bf16)
    tail = total[:, TILE : TILE + 32]
    packed = jnp.concatenate([tail[0:32], tail[32:64], tail[64:96], jnp.zeros((32, 32), f32)], axis=1)
    z_out[SHARE:, :] = packed.astype(bf16)


def scores_kernel(adj2, degree, *refs):
    pieces, out, z_all = refs[:-2], refs[-2], refs[-1]
    me, _ = here()
    for p, piece in enumerate(pieces):
        for b in range(NF):
            src = source(me, SHIFTS[b], SHIFTS[p // 2], lax.rem(me + p, 2))
            src = pl.multiple_of(src * TILE, TILE)
            z_all[pl.ds(src, TILE), :TILE] = piece[b]
            tail = piece[b, SHARE:, :].astype(f32)
            tail = jnp.concatenate([tail[:, 0:32], tail[:, 32:64], tail[:, 64:96], jnp.zeros((32, 32), f32)], axis=0)
            tail = jnp.concatenate([tail, jnp.zeros((TILE, 96), f32)], axis=1)
            z_all[pl.ds(src, TILE), TILE:] = tail.astype(bf16)
    part = jnp.dot(adj2[...], z_all[...], preferred_element_type=f32) / degree[:, :1]
    out[...] = part.T[0:160].astype(bf16)


def sum_kernel(p0, p1, p2, p3, b_out, out):
    total = (p0[...].astype(f32) + p2[...].astype(f32)) + (p1[...].astype(f32) + p3[...].astype(f32))
    bias = jnp.broadcast_to(b_out[...], (TILE, 256)).T[:, 0:1]
    out[...] = total[0:CLS] + bias[0:CLS]


def local(features, counts, tile_mask, w_in, b_in, w_out, b_out):
    adj, adj2, degree = make_adjacency(tile_mask, counts)

    mine = features.T
    ring = [first_axis(mine, s) for s in (1, 3, 2)]
    four = pl.pallas_call(
        stack_kernel, out_shape=jax.ShapeDtypeStruct((NF, 192, ROWS), bf16),
        in_specs=[VM] * 4 + [pl.BlockSpec(memory_space=pl.ANY)], out_specs=VM,
        compiler_params=params(), cost_estimate=cost(1e5, 1.2e6), name="stack",
    )(mine, *ring, degree)
    rows = {t: second_axis(four, t) for t in (1, 3, 2)}

    near, far = pl.pallas_call(
        pack_kernel, out_shape=[jax.ShapeDtypeStruct((256, 512), bf16)] * 2,
        in_specs=[VM] * 3 + [pl.BlockSpec(memory_space=pl.ANY)], out_specs=[VM] * 2,
        compiler_params=params(), cost_estimate=cost(1e5, 1.2e6), name="pack",
    )(w_in, w_out.T, b_in.reshape(1, 256), four)
    near = [near] + [along_feat(near, s) for s in (1, 2, 3)]
    far = [far] + [swap(w) for w in near[1:]]

    total_shape = jax.ShapeDtypeStruct((ROWS, 192), f32)
    pieces = [four, swap(four)]
    total = pl.pallas_call(
        product_first, out_shape=total_shape, in_specs=[VM] * 3, out_specs=VM,
        compiler_params=params(), cost_estimate=blocks_cost(pieces), name="product_first",
    )(adj, *pieces)
    total, rows[2] = lax.optimization_barrier((total, rows[2]))
    pieces = [rows[1], swap(rows[1]), rows[3], swap(rows[3])]
    total = pl.pallas_call(
        product_next, out_shape=total_shape, in_specs=[VM] * 6, out_specs=VM,
        compiler_params=params(), cost_estimate=blocks_cost(pieces), name="product_next",
    )(adj, total, *pieces)
    pieces = [rows[2], swap(rows[2])]
    means = pl.pallas_call(
        product_last, out_shape=[jax.ShapeDtypeStruct((SHARE, 192), bf16)] * NF,
        in_specs=[VM] * 5, out_specs=[VM] * NF,
        scratch_shapes=[pltpu.VMEM((ROWS, 192), f32)],
        compiler_params=params(), cost_estimate=blocks_cost(pieces), name="product_last",
    )(adj, total, degree, *pieces)

    g = [means[0]] + [along_feat(means[s], s) for s in (1, 2, 3)]
    z_block = pl.pallas_call(
        hidden_kernel, out_shape=jax.ShapeDtypeStruct((TILE, TILE), bf16),
        in_specs=[VM] * 12, out_specs=VM,
        scratch_shapes=[pltpu.VMEM((SHARE, 512), f32)],
        compiler_params=params(), cost_estimate=cost(2 * 96 * 768 * 1024, 2e6), name="hidden",
    )(*g, *near, *far)

    z_four = jnp.stack([z_block] + [first_axis(z_block, s) for s in (1, 3, 2)])
    z_rows = [z_four] + [second_axis(z_four, t) for t in (1, 3, 2)]
    z_pieces = [z for row in z_rows for z in (row, swap(row))]
    part = pl.pallas_call(
        scores_kernel, out_shape=jax.ShapeDtypeStruct((160, ROWS), bf16),
        in_specs=[VM] * 10, out_specs=VM,
        scratch_shapes=[pltpu.VMEM((NV * TILE, 256), bf16)],
        compiler_params=params(), cost_estimate=cost(2 * 384 * 4096 * 256, 5e6), name="scores",
    )(adj2, degree, *z_pieces)
    parts = [part] + [along_feat(part, s) for s in (1, 2, 3)]
    return pl.pallas_call(
        sum_kernel, out_shape=jax.ShapeDtypeStruct((CLS, ROWS), f32),
        in_specs=[VM] * 5, out_specs=VM,
        compiler_params=params(), cost_estimate=cost(3e5, 8e5), name="sum",
    )(*parts, jnp.pad(b_out, (0, 256 - CLS)).reshape(1, 256)).T


def solution(mesh):
    placed = (
        P("vert", "feat"),
        P("vert", None),
        P("vert", None),
        P("feat", None),
        P("feat"),
        P("feat", None),
        P(),
    )
    return jax.shard_map(
        local, mesh=mesh, in_specs=placed, out_specs=P("vert", None), check_vma=False
    )
```

```python
import jax
import jax.numpy as jnp
from jax import lax
from jax.experimental import pallas as pl
from jax.experimental.pallas import tpu as pltpu
from jax.sharding import PartitionSpec as P

TILE = 128
ROWS = 384
NV = 32
NF = 4
SHARE = ROWS // NF
CLS = 153
bf16 = jnp.bfloat16
f32 = jnp.float32
NT = (((1,), (1,)), ((), ()))
VM = pl.BlockSpec(memory_space=pltpu.VMEM)
SM = pl.BlockSpec(memory_space=pltpu.SMEM)
ANY = pl.BlockSpec(memory_space=pl.ANY)


def here():
    return lax.axis_index("vert").astype(jnp.int32), lax.axis_index("feat").astype(jnp.int32)


def source(me, s, t, c):
    spot = lax.div(me, 2)
    x, z = lax.div(spot, NF), lax.rem(spot, NF)
    x = lax.rem(x + NF - jnp.where(c == 0, s, t), NF)
    z = lax.rem(z + NF - jnp.where(c == 0, t, s), NF)
    return (x * NF + z) * 2 + c


SHIFTS = (0, 1, 3, 2)


def params(mib=16):
    return pltpu.CompilerParams(vmem_limit_bytes=mib * 2**20)


def cost(flops, nbytes):
    return pl.CostEstimate(flops=int(flops), bytes_accessed=int(nbytes), transcendentals=0)


def positions(move):
    pairs = []
    for x in range(4):
        for z in range(4):
            for c in range(2):
                xx, zz, cc = move(x, z, c)
                pairs.append(((x * 4 + z) * 2 + c, (xx % 4 * 4 + zz % 4) * 2 + cc % 2))
    return pairs


def first_axis(value, shift):
    return lax.ppermute(value, "vert", positions(lambda x, z, c: (x + shift * (1 - c), z + shift * c, c)))


def second_axis(value, shift):
    return lax.ppermute(value, "vert", positions(lambda x, z, c: (x + shift * c, z + shift * (1 - c), c)))


def swap(value):
    return lax.ppermute(value, "vert", positions(lambda x, z, c: (x, z, 1 - c)))


def along_feat(value, shift):
    return lax.ppermute(value, "feat", [(i, (i + shift) % NF) for i in range(NF)])


def both_sides(value):
    pairs = [(f * NV + v, (f + 1 - 2 * (v % 2)) % NF * NV + v) for v in range(NV) for f in range(NF)]
    return lax.ppermute(value, ("feat", "vert"), pairs)


CHUNK = 4 * ROWS
STEPS = NV * ROWS // CHUNK
SLOTS = 3


def adjacency_kernel(mask, counts, *refs):
    adj, adj2, degree, slots, sems = refs[-5:]
    me, feat = here()
    source_row = lax.broadcasted_iota(jnp.int32, (ROWS, TILE), 0)
    target = lax.broadcasted_iota(jnp.int32, (ROWS, TILE), 1)
    chosen = (source_row == target + feat * SHARE) & (target < SHARE)
    pick = (chosen | (target == SHARE)).astype(f32).astype(bf16)
    inside = lax.broadcasted_iota(jnp.int32, (TILE, TILE), 1) < SHARE

    def fetch(step, slot):
        start = pl.multiple_of(step * CHUNK, CHUNK)
        return pltpu.make_async_copy(counts.at[:, pl.ds(start, CHUNK)], slots.at[slot], sems.at[slot])

    for i in range(SLOTS - 1):
        fetch(i, i).start()
    degree[...] = jnp.zeros_like(degree)

    @pl.loop(0, STEPS)
    def _(step):
        slot = lax.rem(step, SLOTS)

        @pl.when(step + SLOTS - 1 < STEPS)
        def _():
            fetch(step + SLOTS - 1, lax.rem(step + SLOTS - 1, SLOTS)).start()

        fetch(step, slot).wait()
        for j in range(CHUNK // ROWS):
            base = pl.multiple_of(step * CHUNK + j * ROWS, ROWS)
            place = pl.multiple_of((step * (CHUNK // ROWS) + j) * TILE, TILE)
            for i in range(ROWS // TILE):
                rows = slice(i * TILE, (i + 1) * TILE)
                strip = []
                for k in range(ROWS // TILE):
                    stored = mask[i, (step * (CHUNK // ROWS) + j) * (ROWS // TILE) + k].astype(f32)
                    tile = slots[slot, rows, j * ROWS + k * TILE : j * ROWS + (k + 1) * TILE]
                    strip.append((tile.astype(f32) * stored).astype(bf16))
                strip = jnp.concatenate(strip, axis=1)
                adj[rows, pl.ds(base, ROWS)] = strip
                part = jnp.dot(strip, pick, preferred_element_type=f32)
                degree[rows, :] += part
                adj2[rows, pl.ds(place, TILE)] = jnp.where(inside, part, 0.0).astype(bf16)

    place = pl.ds(pl.multiple_of(me * TILE, TILE), TILE)
    adj2[:, place] = (adj2[:, place].astype(f32) + chosen.astype(f32)).astype(bf16)
    row = lax.broadcasted_iota(jnp.int32, (ROWS, ROWS), 0)
    col = lax.broadcasted_iota(jnp.int32, (ROWS, ROWS), 1)
    place = pl.ds(pl.multiple_of(me * ROWS, ROWS), ROWS)
    adj[:, place] = (adj[:, place].astype(f32) + (row == col).astype(f32)).astype(bf16)
    degree[...] = jnp.broadcast_to(degree[:, SHARE : SHARE + 1] + 1.0, degree.shape)


def make_adjacency(tile_mask, counts, *after):
    counts = pltpu.with_memory_space_constraint(counts, pltpu.HBM)
    return pl.pallas_call(
        adjacency_kernel,
        in_specs=[SM, pl.BlockSpec(memory_space=pltpu.HBM)] + [ANY] * len(after),
        out_specs=[VM] * 3,
        out_shape=[
            pltpu.VMEM((ROWS, NV * ROWS), bf16),
            pltpu.VMEM((ROWS, NV * TILE), bf16),
            pltpu.VMEM((ROWS, TILE), f32),
        ],
        scratch_shapes=[pltpu.VMEM((SLOTS, ROWS, CHUNK), jnp.int32), pltpu.SemaphoreType.DMA((SLOTS,))],
        compiler_params=params(24),
        cost_estimate=cost(2.4e9, 31e6),
        name="adjacency",
    )(tile_mask, counts, *after)


def pack_kernel(w_in, w_out_t, b_in, whole, mine):
    zero = jnp.zeros((192 - CLS, TILE), f32)
    for half in range(2):
        lanes = slice(TILE * half, TILE * (half + 1))
        for k in range(NF):
            whole[half, 0:192, k * TILE : (k + 1) * TILE] = w_in[:, 256 * k + TILE * half : 256 * k + TILE * (half + 1)]
        w = jnp.concatenate([w_out_t[:, lanes].astype(f32), zero], axis=0)
        for k in range(NF):
            whole[half, 192:240, k * TILE : (k + 1) * TILE] = w[48 * k : 48 * (k + 1)].astype(bf16)
        b = jnp.broadcast_to(b_in[:, lanes], (16, TILE))
        hi = b.astype(bf16).astype(f32)
        mid = (b - hi).astype(bf16).astype(f32)
        low = b - hi - mid
        row = lax.broadcasted_iota(jnp.int32, (16, TILE), 0)
        b = jnp.where(row == 0, hi, jnp.where(row == 1, mid, jnp.where(row == 2, low, 0.0)))
        whole[half, 240:256, 0:TILE] = b.astype(bf16)
        whole[half, 240:256, TILE:] = jnp.zeros((16, 512 - TILE), bf16)
    mine[...] = whole[lax.rem(here()[0], 2)]


def stack_kernel(a, b, c, d, after, after_too, out):
    for i, part in enumerate((a, b, c, d)):
        out[i] = part[...]


def add_blocks(shifts, adj, total, pieces):
    me, _ = here()
    for p, piece in enumerate(pieces):
        core = lax.rem(me + p, 2)
        for b in range(NF):
            src = source(me, SHIFTS[b], shifts[p // 2], core)
            src = pl.multiple_of(src * ROWS, ROWS)
            total = total + lax.dot_general(adj[:, pl.ds(src, ROWS)], piece[b], NT, preferred_element_type=f32)
    return total


def product_first(adj, *refs):
    refs[-1][...] = add_blocks((0,), adj, jnp.zeros(refs[-1].shape, f32), refs[:-1])


def product_next(adj, before, *refs):
    refs[-1][...] = add_blocks((1, 3), adj, before[...], refs[:-1])


def product_last(adj, before, degree, *refs):
    pieces, outs, mean = refs[:-5], refs[-5:-1], refs[-1]
    feat = here()[1]
    total = add_blocks((2,), adj, before[...], pieces)
    mean[...] = total / degree[:, :1]
    for s in range(NF):
        q = lax.rem(feat + s, NF)
        outs[s][...] = mean[pl.ds(pl.multiple_of(q * SHARE, SHARE), SHARE), :].astype(bf16)


def blocks_cost(pieces):
    n = sum(p.shape[0] for p in pieces)
    return cost(2 * 384 * 384 * 256 * n, n * 450e3)


def hidden_kernel(g0, g1, g2, g3, own, side, other_side, near, far, z_out, hid):
    me, feat = here()
    core = lax.rem(me, 2)
    even = core == 0
    ga = jnp.where(even, g1[...].astype(f32), g3[...].astype(f32)).astype(bf16)
    gb = jnp.where(even, g3[...].astype(f32), g1[...].astype(f32)).astype(bf16)
    down, up = lax.rem(feat + NF - 1, NF), lax.rem(feat + 1, NF)
    across = lax.rem(feat + 2, NF)
    total = jnp.zeros((SHARE, 192), f32)
    for half, opposite in ((core, near), (1 - core, far)):
        parts = (
            (g0[...], own.at[half], feat),
            (ga, side.at[half], jnp.where(even, down, up)),
            (gb, other_side.at[half], jnp.where(even, up, down)),
            (g2[...], opposite, across),
        )
        pre = jnp.zeros((SHARE, 512), f32)
        for g, part, _ in parts:
            pre = pre + jnp.dot(g, part[0:192, :], preferred_element_type=f32)
        hid[...] = pre
        for _, part, owner in parts:
            lanes = pl.ds(pl.multiple_of(owner * TILE, TILE), TILE)
            b = part[240:256, 0:TILE].astype(f32)
            bias = b[0:1] + b[1:2] + b[2:3]
            unit = jnp.maximum(hid[:, lanes] + bias, 0.0).astype(bf16)
            w = part[192:240, :]
            w = jnp.concatenate([w[:, k * TILE : (k + 1) * TILE] for k in range(NF)], axis=0)
            total = total + lax.dot_general(unit, w, NT, preferred_element_type=f32)
    z_out[0:SHARE, :] = total[:, :TILE].astype(bf16)
    tail = total[:, TILE : TILE + 32]
    packed = jnp.concatenate([tail[0:32], tail[32:64], tail[64:96], jnp.zeros((32, 32), f32)], axis=1)
    z_out[SHARE:, :] = packed.astype(bf16)


def scores_kernel(adj2, degree, *refs):
    pieces, out, z_all = refs[:-2], refs[-2], refs[-1]
    me, _ = here()
    for p, piece in enumerate(pieces):
        for b in range(NF):
            src = source(me, SHIFTS[b], SHIFTS[p // 2], lax.rem(me + p, 2))
            src = pl.multiple_of(src * TILE, TILE)
            z_all[pl.ds(src, TILE), :TILE] = piece[b]
            tail = piece[b, SHARE:, :].astype(f32)
            tail = jnp.concatenate([tail[:, 0:32], tail[:, 32:64], tail[:, 64:96], jnp.zeros((32, 32), f32)], axis=0)
            tail = jnp.concatenate([tail, jnp.zeros((TILE, 96), f32)], axis=1)
            z_all[pl.ds(src, TILE), TILE:] = tail.astype(bf16)
    part = jnp.dot(adj2[...], z_all[...], preferred_element_type=f32) / degree[:, :1]
    out[...] = part.T[0:160].astype(bf16)


def sum_kernel(p0, p1, p2, p3, b_out, out):
    total = (p0[...].astype(f32) + p2[...].astype(f32)) + (p1[...].astype(f32) + p3[...].astype(f32))
    bias = jnp.broadcast_to(b_out[...], (TILE, 256)).T[:, 0:1]
    out[...] = total[0:CLS] + bias[0:CLS]


def local(features, counts, tile_mask, w_in, b_in, w_out, b_out):
    whole, mine_half = pl.pallas_call(
        pack_kernel,
        out_shape=[jax.ShapeDtypeStruct((2, 256, 512), bf16), jax.ShapeDtypeStruct((256, 512), bf16)],
        in_specs=[VM] * 3, out_specs=[VM] * 2,
        compiler_params=params(), cost_estimate=cost(1e5, 1.2e6), name="pack",
    )(w_in, w_out.T, b_in.reshape(1, 256))
    side = both_sides(whole)
    near = along_feat(mine_half, 2)
    adj, adj2, degree = make_adjacency(tile_mask, counts, mine_half)

    mine = features.T
    ring = [first_axis(mine, s) for s in (1, 3, 2)]
    four = pl.pallas_call(
        stack_kernel, out_shape=jax.ShapeDtypeStruct((NF, 192, ROWS), bf16),
        in_specs=[VM] * 4 + [ANY] * 2, out_specs=VM,
        compiler_params=params(), cost_estimate=cost(1e5, 1.2e6), name="stack",
    )(mine, *ring, degree, side)
    rows = {t: second_axis(four, t) for t in (1, 3, 2)}

    near, rows[3] = lax.optimization_barrier((near, rows[3]))
    other_side, far = swap(side), swap(near)

    total_shape = jax.ShapeDtypeStruct((ROWS, 192), f32)
    pieces = [four, swap(four)]
    total = pl.pallas_call(
        product_first, out_shape=total_shape, in_specs=[VM] * 3, out_specs=VM,
        compiler_params=params(), cost_estimate=blocks_cost(pieces), name="product_first",
    )(adj, *pieces)
    total, rows[2] = lax.optimization_barrier((total, rows[2]))
    pieces = [rows[1], swap(rows[1]), rows[3], swap(rows[3])]
    total = pl.pallas_call(
        product_next, out_shape=total_shape, in_specs=[VM] * 6, out_specs=VM,
        compiler_params=params(), cost_estimate=blocks_cost(pieces), name="product_next",
    )(adj, total, *pieces)
    pieces = [rows[2], swap(rows[2])]
    means = pl.pallas_call(
        product_last, out_shape=[jax.ShapeDtypeStruct((SHARE, 192), bf16)] * NF,
        in_specs=[VM] * 5, out_specs=[VM] * NF,
        scratch_shapes=[pltpu.VMEM((ROWS, 192), f32)],
        compiler_params=params(), cost_estimate=blocks_cost(pieces), name="product_last",
    )(adj, total, degree, *pieces)

    g = [means[0]] + [along_feat(means[s], s) for s in (1, 2, 3)]
    z_block = pl.pallas_call(
        hidden_kernel, out_shape=jax.ShapeDtypeStruct((TILE, TILE), bf16),
        in_specs=[VM] * 9, out_specs=VM,
        scratch_shapes=[pltpu.VMEM((SHARE, 512), f32)],
        compiler_params=params(), cost_estimate=cost(2 * 96 * 768 * 1024, 2e6), name="hidden",
    )(*g, whole, side, other_side, near, far)

    z_four = jnp.stack([z_block] + [first_axis(z_block, s) for s in (1, 3, 2)])
    z_rows = [z_four] + [second_axis(z_four, t) for t in (1, 3, 2)]
    z_pieces = [z for row in z_rows for z in (row, swap(row))]
    part = pl.pallas_call(
        scores_kernel, out_shape=jax.ShapeDtypeStruct((160, ROWS), bf16),
        in_specs=[VM] * 10, out_specs=VM,
        scratch_shapes=[pltpu.VMEM((NV * TILE, 256), bf16)],
        compiler_params=params(), cost_estimate=cost(2 * 384 * 4096 * 256, 5e6), name="scores",
    )(adj2, degree, *z_pieces)
    parts = [part] + [along_feat(part, s) for s in (1, 2, 3)]
    return pl.pallas_call(
        sum_kernel, out_shape=jax.ShapeDtypeStruct((CLS, ROWS), f32),
        in_specs=[VM] * 5, out_specs=VM,
        compiler_params=params(), cost_estimate=cost(3e5, 8e5), name="sum",
    )(*parts, jnp.pad(b_out, (0, 256 - CLS)).reshape(1, 256)).T


def solution(mesh):
    placed = (
        P("vert", "feat"),
        P("vert", None),
        P("vert", None),
        P("feat", None),
        P("feat"),
        P("feat", None),
        P(),
    )
    return jax.shard_map(
        local, mesh=mesh, in_specs=placed, out_specs=P("vert", None), check_vma=False
    )
```

```python
import functools

import jax
import jax.numpy as jnp
from jax import lax
from jax.experimental import pallas as pl
from jax.experimental.pallas import tpu as pltpu
from jax.sharding import PartitionSpec as P

TILE = 128
ROWS = 384
NV = 32
NF = 4
SHARE = ROWS // NF
CLS = 153
bf16 = jnp.bfloat16
f32 = jnp.float32
NT = (((1,), (1,)), ((), ()))
VM = pl.BlockSpec(memory_space=pltpu.VMEM)
SM = pl.BlockSpec(memory_space=pltpu.SMEM)
HB = pl.BlockSpec(memory_space=pltpu.HBM)
ANY = pl.BlockSpec(memory_space=pl.ANY)


def here():
    return lax.axis_index("vert").astype(jnp.int32), lax.axis_index("feat").astype(jnp.int32)


def source(me, s, t, c):
    spot = lax.div(me, 2)
    x, z = lax.div(spot, NF), lax.rem(spot, NF)
    x = lax.rem(x + NF - jnp.where(c == 0, s, t), NF)
    z = lax.rem(z + NF - jnp.where(c == 0, t, s), NF)
    return (x * NF + z) * 2 + c


SHIFTS = (0, 1, 3, 2)


def params(mib=16):
    return pltpu.CompilerParams(vmem_limit_bytes=mib * 2**20)


def cost(flops, nbytes):
    return pl.CostEstimate(flops=int(flops), bytes_accessed=int(nbytes), transcendentals=0)


def positions(move):
    pairs = []
    for x in range(4):
        for z in range(4):
            for c in range(2):
                xx, zz, cc = move(x, z, c)
                pairs.append(((x * 4 + z) * 2 + c, (xx % 4 * 4 + zz % 4) * 2 + cc % 2))
    return pairs


def first_axis(value, shift):
    return lax.ppermute(value, "vert", positions(lambda x, z, c: (x + shift * (1 - c), z + shift * c, c)))


def second_axis(value, shift):
    return lax.ppermute(value, "vert", positions(lambda x, z, c: (x + shift * c, z + shift * (1 - c), c)))


def swap(value):
    return lax.ppermute(value, "vert", positions(lambda x, z, c: (x, z, 1 - c)))


def along_feat(value, shift):
    return lax.ppermute(value, "feat", [(i, (i + shift) % NF) for i in range(NF)])


def both_sides(value):
    pairs = [(f * NV + v, (f + 1 - 2 * (v % 2)) % NF * NV + v) for v in range(NV) for f in range(NF)]
    return lax.ppermute(value, ("feat", "vert"), pairs)


CHUNK = 4 * ROWS
STEPS = NV * ROWS // CHUNK
SLOTS = 3


def adjacency_kernel(part, mask, counts, *refs):
    if part == 0:
        w_in, w_out_t, b_in, adj, adj2, degree, whole, mine, slots, sems, mask_sm, one, w1, w2, b1, three = refs
        extra = [(w_in, w1), (w_out_t, w2), (b_in, b1)]
    else:
        adj, adj2, degree, slots, sems, mask_sm, one = refs[4:]
        extra = []
    me, feat = here()
    first, last = part * STEPS // 2, (part + 1) * STEPS // 2
    mask_copy = pltpu.make_async_copy(mask, mask_sm, one)
    mask_copy.start()
    source_row = lax.broadcasted_iota(jnp.int32, (ROWS, TILE), 0)
    target = lax.broadcasted_iota(jnp.int32, (ROWS, TILE), 1)
    chosen = (source_row == target + feat * SHARE) & (target < SHARE)
    pick = (chosen | (target == SHARE)).astype(f32).astype(bf16)
    inside = lax.broadcasted_iota(jnp.int32, (TILE, TILE), 1) < SHARE

    def fetch(step, slot):
        start = pl.multiple_of(step * CHUNK, CHUNK)
        return pltpu.make_async_copy(counts.at[:, pl.ds(start, CHUNK)], slots.at[slot], sems.at[slot])

    for i in range(SLOTS - 1):
        fetch(first + i, i).start()
    extra = [pltpu.make_async_copy(a, b, three.at[i]) for i, (a, b) in enumerate(extra)]
    for copy in extra:
        copy.start()
    if part == 0:
        degree[...] = jnp.zeros_like(degree)
    mask_copy.wait()

    @pl.loop(first, last)
    def _(step):
        slot = lax.rem(step - first, SLOTS)

        @pl.when(step + SLOTS - 1 < last)
        def _():
            fetch(step + SLOTS - 1, lax.rem(step - first + SLOTS - 1, SLOTS)).start()

        fetch(step, slot).wait()
        for j in range(CHUNK // ROWS):
            base = pl.multiple_of(step * CHUNK + j * ROWS, ROWS)
            place = pl.multiple_of((step * (CHUNK // ROWS) + j) * TILE, TILE)
            for i in range(ROWS // TILE):
                rows = slice(i * TILE, (i + 1) * TILE)
                strip = []
                for k in range(ROWS // TILE):
                    stored = mask_sm[i, (step * (CHUNK // ROWS) + j) * (ROWS // TILE) + k].astype(f32)
                    tile = slots[slot, rows, j * ROWS + k * TILE : j * ROWS + (k + 1) * TILE]
                    strip.append((tile.astype(f32) * stored).astype(bf16))
                strip = jnp.concatenate(strip, axis=1)
                adj[rows, pl.ds(base, ROWS)] = strip
                part = jnp.dot(strip, pick, preferred_element_type=f32)
                degree[rows, :] += part
                adj2[rows, pl.ds(place, TILE)] = jnp.where(inside, part, 0.0).astype(bf16)

    for copy in extra:
        copy.wait()
    if part == 0:
        pack(w1, w2, b1, whole, mine)
        return
    place = pl.ds(pl.multiple_of(me * TILE, TILE), TILE)
    adj2[:, place] = (adj2[:, place].astype(f32) + chosen.astype(f32)).astype(bf16)
    row = lax.broadcasted_iota(jnp.int32, (ROWS, ROWS), 0)
    col = lax.broadcasted_iota(jnp.int32, (ROWS, ROWS), 1)
    place = pl.ds(pl.multiple_of(me * ROWS, ROWS), ROWS)
    adj[:, place] = (adj[:, place].astype(f32) + (row == col).astype(f32)).astype(bf16)
    degree[...] = jnp.broadcast_to(degree[:, SHARE : SHARE + 1] + 1.0, degree.shape)


ADJACENCY = [
    pltpu.VMEM((ROWS, NV * ROWS), bf16),
    pltpu.VMEM((ROWS, NV * TILE), bf16),
    pltpu.VMEM((ROWS, TILE), f32),
]
ADJACENCY_SCRATCH = [
    pltpu.VMEM((SLOTS, ROWS, CHUNK), jnp.int32),
    pltpu.SemaphoreType.DMA((SLOTS,)),
    pltpu.SMEM((ROWS // TILE, NV * ROWS // TILE), jnp.int32),
    pltpu.SemaphoreType.DMA(()),
]


def first_half(tile_mask, counts, w_in, w_out_t, b_in):
    return pl.pallas_call(
        functools.partial(adjacency_kernel, 0),
        in_specs=[HB] * 5,
        out_specs=[VM] * 5,
        out_shape=ADJACENCY + [
            jax.ShapeDtypeStruct((2, 256, 512), bf16),
            jax.ShapeDtypeStruct((256, 512), bf16),
        ],
        scratch_shapes=ADJACENCY_SCRATCH + [
            pltpu.VMEM((192, 1024), bf16),
            pltpu.VMEM((CLS, 256), bf16),
            pltpu.VMEM((1, 256), f32),
            pltpu.SemaphoreType.DMA((3,)),
        ],
        compiler_params=params(24),
        cost_estimate=cost(1.2e9, 16e6),
        name="adjacency_first",
    )(tile_mask, counts, w_in, w_out_t, b_in)


def second_half(tile_mask, counts, adj, adj2, degree, after):
    return pl.pallas_call(
        functools.partial(adjacency_kernel, 1),
        in_specs=[HB] * 2 + [VM] * 3 + [ANY],
        out_specs=[VM] * 3,
        out_shape=ADJACENCY,
        input_output_aliases={2: 0, 3: 1, 4: 2},
        scratch_shapes=ADJACENCY_SCRATCH,
        compiler_params=params(24),
        cost_estimate=cost(1.2e9, 16e6),
        name="adjacency_second",
    )(tile_mask, counts, adj, adj2, degree, after)


def pack(w_in, w_out_t, b_in, whole, mine):
    zero = jnp.zeros((192 - CLS, TILE), f32)
    for half in range(2):
        lanes = slice(TILE * half, TILE * (half + 1))
        for k in range(NF):
            whole[half, 0:192, k * TILE : (k + 1) * TILE] = w_in[:, 256 * k + TILE * half : 256 * k + TILE * (half + 1)]
        w = jnp.concatenate([w_out_t[:, lanes].astype(f32), zero], axis=0)
        for k in range(NF):
            whole[half, 192:240, k * TILE : (k + 1) * TILE] = w[48 * k : 48 * (k + 1)].astype(bf16)
        b = jnp.broadcast_to(b_in[:, lanes], (16, TILE))
        hi = b.astype(bf16).astype(f32)
        mid = (b - hi).astype(bf16).astype(f32)
        low = b - hi - mid
        row = lax.broadcasted_iota(jnp.int32, (16, TILE), 0)
        b = jnp.where(row == 0, hi, jnp.where(row == 1, mid, jnp.where(row == 2, low, 0.0)))
        whole[half, 240:256, 0:TILE] = b.astype(bf16)
        whole[half, 240:256, TILE:] = jnp.zeros((16, 512 - TILE), bf16)
    mine[...] = whole[lax.rem(here()[0], 2)]


def stack_kernel(a, b, c, d, after, out):
    for i, part in enumerate((a, b, c, d)):
        out[i] = part[...]


def add_blocks(shifts, adj, total, pieces):
    me, _ = here()
    for p, piece in enumerate(pieces):
        core = lax.rem(me + p, 2)
        for b in range(NF):
            src = source(me, SHIFTS[b], shifts[p // 2], core)
            src = pl.multiple_of(src * ROWS, ROWS)
            total = total + lax.dot_general(adj[:, pl.ds(src, ROWS)], piece[b], NT, preferred_element_type=f32)
    return total


def product_first(adj, *refs):
    refs[-1][...] = add_blocks((0,), adj, jnp.zeros(refs[-1].shape, f32), refs[:-2])


def product_next(adj, before, *refs):
    refs[-1][...] = add_blocks((1, 3), adj, before[...], refs[:-1])


def product_last(adj, before, degree, *refs):
    pieces, outs, mean = refs[:-5], refs[-5:-1], refs[-1]
    feat = here()[1]
    total = add_blocks((2,), adj, before[...], pieces)
    mean[...] = total / degree[:, :1]
    for s in range(NF):
        q = lax.rem(feat + s, NF)
        outs[s][...] = mean[pl.ds(pl.multiple_of(q * SHARE, SHARE), SHARE), :].astype(bf16)


def blocks_cost(pieces):
    n = sum(p.shape[0] for p in pieces)
    return cost(2 * 384 * 384 * 256 * n, n * 450e3)


def hidden_kernel(g0, g1, g2, g3, own, side, other_side, near, far, z_out, hid):
    me, feat = here()
    core = lax.rem(me, 2)
    even = core == 0
    ga = jnp.where(even, g1[...].astype(f32), g3[...].astype(f32)).astype(bf16)
    gb = jnp.where(even, g3[...].astype(f32), g1[...].astype(f32)).astype(bf16)
    down, up = lax.rem(feat + NF - 1, NF), lax.rem(feat + 1, NF)
    across = lax.rem(feat + 2, NF)
    total = jnp.zeros((SHARE, 192), f32)
    for half, opposite in ((core, near), (1 - core, far)):
        parts = (
            (g0[...], own.at[half], feat),
            (ga, side.at[half], jnp.where(even, down, up)),
            (gb, other_side.at[half], jnp.where(even, up, down)),
            (g2[...], opposite, across),
        )
        pre = jnp.zeros((SHARE, 512), f32)
        for g, part, _ in parts:
            pre = pre + jnp.dot(g, part[0:192, :], preferred_element_type=f32)
        hid[...] = pre
        for _, part, owner in parts:
            lanes = pl.ds(pl.multiple_of(owner * TILE, TILE), TILE)
            b = part[240:256, 0:TILE].astype(f32)
            bias = b[0:1] + b[1:2] + b[2:3]
            unit = jnp.maximum(hid[:, lanes] + bias, 0.0).astype(bf16)
            w = part[192:240, :]
            w = jnp.concatenate([w[:, k * TILE : (k + 1) * TILE] for k in range(NF)], axis=0)
            total = total + lax.dot_general(unit, w, NT, preferred_element_type=f32)
    z_out[0:SHARE, :] = total[:, :TILE].astype(bf16)
    tail = total[:, TILE : TILE + 32]
    packed = jnp.concatenate([tail[0:32], tail[32:64], tail[64:96], jnp.zeros((32, 32), f32)], axis=1)
    z_out[SHARE:, :] = packed.astype(bf16)


def scores_kernel(adj2, degree, *refs):
    pieces, out, z_all = refs[:-2], refs[-2], refs[-1]
    me, _ = here()
    for p, piece in enumerate(pieces):
        for b in range(NF):
            src = source(me, SHIFTS[b], SHIFTS[p // 2], lax.rem(me + p, 2))
            src = pl.multiple_of(src * TILE, TILE)
            z_all[pl.ds(src, TILE), :TILE] = piece[b]
            tail = piece[b, SHARE:, :].astype(f32)
            tail = jnp.concatenate([tail[:, 0:32], tail[:, 32:64], tail[:, 64:96], jnp.zeros((32, 32), f32)], axis=0)
            tail = jnp.concatenate([tail, jnp.zeros((TILE, 96), f32)], axis=1)
            z_all[pl.ds(src, TILE), TILE:] = tail.astype(bf16)
    part = jnp.dot(adj2[...], z_all[...], preferred_element_type=f32) / degree[:, :1]
    out[...] = part.T[0:160].astype(bf16)


def sum_kernel(p0, p1, p2, p3, b_out, out):
    total = (p0[...].astype(f32) + p2[...].astype(f32)) + (p1[...].astype(f32) + p3[...].astype(f32))
    bias = jnp.broadcast_to(b_out[...], (TILE, 256)).T[:, 0:1]
    out[...] = total[0:CLS] + bias[0:CLS]


def local(features, counts, tile_mask, w_in, b_in, w_out, b_out):
    tile_mask, counts, *weights = (
        pltpu.with_memory_space_constraint(a, pltpu.HBM)
        for a in (tile_mask, counts, w_in, w_out.T, b_in.reshape(1, 256))
    )
    *adjacency, whole, mine_half = first_half(tile_mask, counts, *weights)
    side = both_sides(whole)
    near = along_feat(mine_half, 2)

    mine = features.T
    ring = [first_axis(mine, s) for s in (2, 1, 3)]
    four = pl.pallas_call(
        stack_kernel, out_shape=jax.ShapeDtypeStruct((NF, 192, ROWS), bf16),
        in_specs=[VM] * 4 + [ANY], out_specs=VM,
        compiler_params=params(), cost_estimate=cost(1e5, 1.2e6), name="stack",
    )(mine, ring[1], ring[2], ring[0], mine_half)
    rows = {t: second_axis(four, t) for t in (2, 1, 3)}

    adj, adj2, degree = second_half(tile_mask, counts, *adjacency, mine_half)

    total_shape = jax.ShapeDtypeStruct((ROWS, 192), f32)
    pieces = [four, swap(four)]
    total = pl.pallas_call(
        product_first, out_shape=total_shape, in_specs=[VM] * 3 + [ANY], out_specs=VM,
        compiler_params=params(), cost_estimate=blocks_cost(pieces), name="product_first",
    )(adj, *pieces, near)
    for t in (1, 2, 3):
        rows[t] = lax.optimization_barrier((total, rows[t]))[1]
    side, near, _ = lax.optimization_barrier((side, near, total))
    other_side, far = swap(side), swap(near)
    pieces = [rows[1], swap(rows[1]), rows[3], swap(rows[3])]
    total = pl.pallas_call(
        product_next, out_shape=total_shape, in_specs=[VM] * 6, out_specs=VM,
        compiler_params=params(), cost_estimate=blocks_cost(pieces), name="product_next",
    )(adj, total, *pieces)
    pieces = [rows[2], swap(rows[2])]
    means = pl.pallas_call(
        product_last, out_shape=[jax.ShapeDtypeStruct((SHARE, 192), bf16)] * NF,
        in_specs=[VM] * 5, out_specs=[VM] * NF,
        scratch_shapes=[pltpu.VMEM((ROWS, 192), f32)],
        compiler_params=params(), cost_estimate=blocks_cost(pieces), name="product_last",
    )(adj, total, degree, *pieces)

    g = [means[0]] + [along_feat(means[s], s) for s in (1, 2, 3)]
    z_block = pl.pallas_call(
        hidden_kernel, out_shape=jax.ShapeDtypeStruct((TILE, TILE), bf16),
        in_specs=[VM] * 9, out_specs=VM,
        scratch_shapes=[pltpu.VMEM((SHARE, 512), f32)],
        compiler_params=params(), cost_estimate=cost(2 * 96 * 768 * 1024, 2e6), name="hidden",
    )(*g, whole, side, other_side, near, far)

    z_four = jnp.stack([z_block] + [first_axis(z_block, s) for s in (1, 3, 2)])
    z_rows = [z_four] + [second_axis(z_four, t) for t in (1, 3, 2)]
    z_pieces = [z for row in z_rows for z in (row, swap(row))]
    part = pl.pallas_call(
        scores_kernel, out_shape=jax.ShapeDtypeStruct((160, ROWS), bf16),
        in_specs=[VM] * 10, out_specs=VM,
        scratch_shapes=[pltpu.VMEM((NV * TILE, 256), bf16)],
        compiler_params=params(), cost_estimate=cost(2 * 384 * 4096 * 256, 5e6), name="scores",
    )(adj2, degree, *z_pieces)
    parts = [part] + [along_feat(part, s) for s in (1, 2, 3)]
    return pl.pallas_call(
        sum_kernel, out_shape=jax.ShapeDtypeStruct((CLS, ROWS), f32),
        in_specs=[VM] * 5, out_specs=VM,
        compiler_params=params(), cost_estimate=cost(3e5, 8e5), name="sum",
    )(*parts, jnp.pad(b_out, (0, 256 - CLS)).reshape(1, 256)).T


def solution(mesh):
    placed = (
        P("vert", "feat"),
        P("vert", None),
        P("vert", None),
        P("feat", None),
        P("feat"),
        P("feat", None),
        P(),
    )
    return jax.shard_map(
        local, mesh=mesh, in_specs=placed, out_specs=P("vert", None), check_vma=False
    )
```

```python
import functools

import jax
import jax.numpy as jnp
from jax import lax
from jax.experimental import pallas as pl
from jax.experimental.pallas import tpu as pltpu
from jax.sharding import PartitionSpec as P

TILE = 128
ROWS = 384
NV = 32
NF = 4
SHARE = ROWS // NF
CLS = 153
bf16 = jnp.bfloat16
f32 = jnp.float32
NT = (((1,), (1,)), ((), ()))
VM = pl.BlockSpec(memory_space=pltpu.VMEM)
SM = pl.BlockSpec(memory_space=pltpu.SMEM)
HB = pl.BlockSpec(memory_space=pltpu.HBM)
ANY = pl.BlockSpec(memory_space=pl.ANY)


def here():
    return lax.axis_index("vert").astype(jnp.int32), lax.axis_index("feat").astype(jnp.int32)


def source(me, s, t, c):
    spot = lax.div(me, 2)
    x, z = lax.div(spot, NF), lax.rem(spot, NF)
    x = lax.rem(x + NF - jnp.where(c == 0, s, t), NF)
    z = lax.rem(z + NF - jnp.where(c == 0, t, s), NF)
    return (x * NF + z) * 2 + c


SHIFTS = (0, 2, 1, 3)


def params(mib=16):
    return pltpu.CompilerParams(vmem_limit_bytes=mib * 2**20)


def cost(flops, nbytes):
    return pl.CostEstimate(flops=int(flops), bytes_accessed=int(nbytes), transcendentals=0)


def positions(move):
    pairs = []
    for x in range(4):
        for z in range(4):
            for c in range(2):
                xx, zz, cc = move(x, z, c)
                pairs.append(((x * 4 + z) * 2 + c, (xx % 4 * 4 + zz % 4) * 2 + cc % 2))
    return pairs


def first_axis(value, shift):
    return lax.ppermute(value, "vert", positions(lambda x, z, c: (x + shift * (1 - c), z + shift * c, c)))


def second_axis(value, shift):
    return lax.ppermute(value, "vert", positions(lambda x, z, c: (x + shift * c, z + shift * (1 - c), c)))


def swap(value):
    return lax.ppermute(value, "vert", positions(lambda x, z, c: (x, z, 1 - c)))


def along_feat(value, shift):
    return lax.ppermute(value, "feat", [(i, (i + shift) % NF) for i in range(NF)])


def both_sides(value):
    pairs = [(f * NV + v, (f + 1 - 2 * (v % 2)) % NF * NV + v) for v in range(NV) for f in range(NF)]
    return lax.ppermute(value, ("feat", "vert"), pairs)


CHUNK = 4 * ROWS
STEPS = NV * ROWS // CHUNK
SLOTS = 3
SPLIT = 3


def adjacency_kernel(part, mask, counts, *refs):
    if part == 0:
        w_in, w_out_t, b_in, adj, adj2, degree, whole, mine, slots, sems, mask_sm, one, w1, w2, b1, three = refs
        extra = [(w_in, w1), (w_out_t, w2), (b_in, b1)]
    else:
        adj, adj2, degree, slots, sems, mask_sm, one = refs[4:]
        extra = []
    me, feat = here()
    first, last = (0, SPLIT) if part == 0 else (SPLIT, STEPS)
    mask_copy = pltpu.make_async_copy(mask, mask_sm, one)
    mask_copy.start()
    source_row = lax.broadcasted_iota(jnp.int32, (ROWS, TILE), 0)
    target = lax.broadcasted_iota(jnp.int32, (ROWS, TILE), 1)
    chosen = (source_row == target + feat * SHARE) & (target < SHARE)
    pick = (chosen | (target == SHARE)).astype(f32).astype(bf16)
    inside = lax.broadcasted_iota(jnp.int32, (TILE, TILE), 1) < SHARE

    def fetch(step, slot):
        start = pl.multiple_of(step * CHUNK, CHUNK)
        return pltpu.make_async_copy(counts.at[:, pl.ds(start, CHUNK)], slots.at[slot], sems.at[slot])

    for i in range(SLOTS - 1):
        fetch(first + i, i).start()
    extra = [pltpu.make_async_copy(a, b, three.at[i]) for i, (a, b) in enumerate(extra)]
    for copy in extra:
        copy.start()
    if part == 0:
        degree[...] = jnp.zeros_like(degree)
    mask_copy.wait()

    @pl.loop(first, last)
    def _(step):
        slot = lax.rem(step - first, SLOTS)

        @pl.when(step + SLOTS - 1 < last)
        def _():
            fetch(step + SLOTS - 1, lax.rem(step - first + SLOTS - 1, SLOTS)).start()

        fetch(step, slot).wait()
        for j in range(CHUNK // ROWS):
            base = pl.multiple_of(step * CHUNK + j * ROWS, ROWS)
            place = pl.multiple_of((step * (CHUNK // ROWS) + j) * TILE, TILE)
            for i in range(ROWS // TILE):
                rows = slice(i * TILE, (i + 1) * TILE)
                strip = []
                for k in range(ROWS // TILE):
                    stored = mask_sm[i, (step * (CHUNK // ROWS) + j) * (ROWS // TILE) + k].astype(f32)
                    tile = slots[slot, rows, j * ROWS + k * TILE : j * ROWS + (k + 1) * TILE]
                    strip.append((tile.astype(f32) * stored).astype(bf16))
                strip = jnp.concatenate(strip, axis=1)
                adj[rows, pl.ds(base, ROWS)] = strip
                part = jnp.dot(strip, pick, preferred_element_type=f32)
                degree[rows, :] += part
                adj2[rows, pl.ds(place, TILE)] = jnp.where(inside, part, 0.0).astype(bf16)

    for copy in extra:
        copy.wait()
    if part == 0:
        pack(w1, w2, b1, whole, mine)
        return
    place = pl.ds(pl.multiple_of(me * TILE, TILE), TILE)
    adj2[:, place] = (adj2[:, place].astype(f32) + chosen.astype(f32)).astype(bf16)
    row = lax.broadcasted_iota(jnp.int32, (ROWS, ROWS), 0)
    col = lax.broadcasted_iota(jnp.int32, (ROWS, ROWS), 1)
    place = pl.ds(pl.multiple_of(me * ROWS, ROWS), ROWS)
    adj[:, place] = (adj[:, place].astype(f32) + (row == col).astype(f32)).astype(bf16)
    degree[...] = jnp.broadcast_to(degree[:, SHARE : SHARE + 1] + 1.0, degree.shape)


ADJACENCY = [
    pltpu.VMEM((ROWS, NV * ROWS), bf16),
    pltpu.VMEM((ROWS, NV * TILE), bf16),
    pltpu.VMEM((ROWS, TILE), f32),
]
ADJACENCY_SCRATCH = [
    pltpu.VMEM((SLOTS, ROWS, CHUNK), jnp.int32),
    pltpu.SemaphoreType.DMA((SLOTS,)),
    pltpu.SMEM((ROWS // TILE, NV * ROWS // TILE), jnp.int32),
    pltpu.SemaphoreType.DMA(()),
]


def first_half(tile_mask, counts, w_in, w_out_t, b_in):
    return pl.pallas_call(
        functools.partial(adjacency_kernel, 0),
        in_specs=[HB] * 5,
        out_specs=[VM] * 5,
        out_shape=ADJACENCY + [
            jax.ShapeDtypeStruct((2, 256, 512), bf16),
            jax.ShapeDtypeStruct((256, 512), bf16),
        ],
        scratch_shapes=ADJACENCY_SCRATCH + [
            pltpu.VMEM((192, 1024), bf16),
            pltpu.VMEM((CLS, 256), bf16),
            pltpu.VMEM((1, 256), f32),
            pltpu.SemaphoreType.DMA((3,)),
        ],
        compiler_params=params(24),
        cost_estimate=cost(1.2e9, 16e6),
        name="adjacency_first",
    )(tile_mask, counts, w_in, w_out_t, b_in)


def second_half(tile_mask, counts, adj, adj2, degree, after):
    return pl.pallas_call(
        functools.partial(adjacency_kernel, 1),
        in_specs=[HB] * 2 + [VM] * 3 + [ANY],
        out_specs=[VM] * 3,
        out_shape=ADJACENCY,
        input_output_aliases={2: 0, 3: 1, 4: 2},
        scratch_shapes=ADJACENCY_SCRATCH,
        compiler_params=params(24),
        cost_estimate=cost(1.2e9, 16e6),
        name="adjacency_second",
    )(tile_mask, counts, adj, adj2, degree, after)


def pack(w_in, w_out_t, b_in, whole, mine):
    zero = jnp.zeros((192 - CLS, TILE), f32)
    for half in range(2):
        lanes = slice(TILE * half, TILE * (half + 1))
        for k in range(NF):
            whole[half, 0:192, k * TILE : (k + 1) * TILE] = w_in[:, 256 * k + TILE * half : 256 * k + TILE * (half + 1)]
        w = jnp.concatenate([w_out_t[:, lanes].astype(f32), zero], axis=0)
        for k in range(NF):
            whole[half, 192:240, k * TILE : (k + 1) * TILE] = w[48 * k : 48 * (k + 1)].astype(bf16)
        b = jnp.broadcast_to(b_in[:, lanes], (16, TILE))
        hi = b.astype(bf16).astype(f32)
        mid = (b - hi).astype(bf16).astype(f32)
        low = b - hi - mid
        row = lax.broadcasted_iota(jnp.int32, (16, TILE), 0)
        b = jnp.where(row == 0, hi, jnp.where(row == 1, mid, jnp.where(row == 2, low, 0.0)))
        whole[half, 240:256, 0:TILE] = b.astype(bf16)
        whole[half, 240:256, TILE:] = jnp.zeros((16, 512 - TILE), bf16)
    mine[...] = whole[lax.rem(here()[0], 2)]


def stack_kernel(a, b, c, d, after, out):
    for i, part in enumerate((a, b, c, d)):
        out[i] = part[...]


def add_blocks(kinds, adj, total, pieces):
    me, _ = here()
    for (shift, p), piece in zip(kinds, pieces, strict=True):
        core = lax.rem(me + p, 2)
        for b in range(NF):
            src = source(me, SHIFTS[b], shift, core)
            src = pl.multiple_of(src * ROWS, ROWS)
            total = total + lax.dot_general(adj[:, pl.ds(src, ROWS)], piece[b], NT, preferred_element_type=f32)
    return total


def product_first(kinds, adj, *refs):
    refs[-1][...] = add_blocks(kinds, adj, jnp.zeros(refs[-1].shape, f32), refs[: len(kinds)])


def product_next(kinds, adj, before, *refs):
    refs[-1][...] = add_blocks(kinds, adj, before[...], refs[: len(kinds)])


def product_last(kinds, adj, before, degree, *refs):
    pieces, outs, mean = refs[:-5], refs[-5:-1], refs[-1]
    feat = here()[1]
    total = add_blocks(kinds, adj, before[...], pieces)
    mean[...] = total / degree[:, :1]
    for s in range(NF):
        q = lax.rem(feat + s, NF)
        outs[s][...] = mean[pl.ds(pl.multiple_of(q * SHARE, SHARE), SHARE), :].astype(bf16)


def blocks_cost(pieces):
    n = sum(p.shape[0] for p in pieces)
    return cost(2 * 384 * 384 * 256 * n, n * 450e3)


def hidden_kernel(g0, g1, g2, g3, own, side, other_side, near, far, z_out, hid):
    me, feat = here()
    core = lax.rem(me, 2)
    even = core == 0
    ga = jnp.where(even, g1[...].astype(f32), g3[...].astype(f32)).astype(bf16)
    gb = jnp.where(even, g3[...].astype(f32), g1[...].astype(f32)).astype(bf16)
    down, up = lax.rem(feat + NF - 1, NF), lax.rem(feat + 1, NF)
    across = lax.rem(feat + 2, NF)
    total = jnp.zeros((SHARE, 192), f32)
    for half, opposite in ((core, near), (1 - core, far)):
        parts = (
            (g0[...], own.at[half], feat),
            (ga, side.at[half], jnp.where(even, down, up)),
            (gb, other_side.at[half], jnp.where(even, up, down)),
            (g2[...], opposite, across),
        )
        pre = jnp.zeros((SHARE, 512), f32)
        for g, part, _ in parts:
            pre = pre + jnp.dot(g, part[0:192, :], preferred_element_type=f32)
        hid[...] = pre
        for _, part, owner in parts:
            lanes = pl.ds(pl.multiple_of(owner * TILE, TILE), TILE)
            b = part[240:256, 0:TILE].astype(f32)
            bias = b[0:1] + b[1:2] + b[2:3]
            unit = jnp.maximum(hid[:, lanes] + bias, 0.0).astype(bf16)
            w = part[192:240, :]
            w = jnp.concatenate([w[:, k * TILE : (k + 1) * TILE] for k in range(NF)], axis=0)
            total = total + lax.dot_general(unit, w, NT, preferred_element_type=f32)
    z_out[0:SHARE, :] = total[:, :TILE].astype(bf16)
    tail = total[:, TILE : TILE + 32]
    packed = jnp.concatenate([tail[0:32], tail[32:64], tail[64:96], jnp.zeros((32, 32), f32)], axis=1)
    z_out[SHARE:, :] = packed.astype(bf16)


def scores_kernel(adj2, degree, *refs):
    pieces, out, z_all = refs[:-2], refs[-2], refs[-1]
    me, _ = here()
    for p, piece in enumerate(pieces):
        for b in range(NF):
            src = source(me, SHIFTS[b], SHIFTS[p // 2], lax.rem(me + p, 2))
            src = pl.multiple_of(src * TILE, TILE)
            z_all[pl.ds(src, TILE), :TILE] = piece[b]
            tail = piece[b, SHARE:, :].astype(f32)
            tail = jnp.concatenate([tail[:, 0:32], tail[:, 32:64], tail[:, 64:96], jnp.zeros((32, 32), f32)], axis=0)
            tail = jnp.concatenate([tail, jnp.zeros((TILE, 96), f32)], axis=1)
            z_all[pl.ds(src, TILE), TILE:] = tail.astype(bf16)
    part = jnp.dot(adj2[...], z_all[...], preferred_element_type=f32) / degree[:, :1]
    out[...] = part.T[0:160].astype(bf16)


def sum_kernel(p0, p1, p2, p3, b_out, out):
    total = (p0[...].astype(f32) + p2[...].astype(f32)) + (p1[...].astype(f32) + p3[...].astype(f32))
    bias = jnp.broadcast_to(b_out[...], (TILE, 256)).T[:, 0:1]
    out[...] = total[0:CLS] + bias[0:CLS]


def local(features, counts, tile_mask, w_in, b_in, w_out, b_out):
    tile_mask, counts, *weights = (
        pltpu.with_memory_space_constraint(a, pltpu.HBM)
        for a in (tile_mask, counts, w_in, w_out.T, b_in.reshape(1, 256))
    )
    *adjacency, whole, mine_half = first_half(tile_mask, counts, *weights)
    near = along_feat(mine_half, 2)

    mine = features.T
    ring = [first_axis(mine, s) for s in (2, 1, 3)]
    four = pl.pallas_call(
        stack_kernel, out_shape=jax.ShapeDtypeStruct((NF, 192, ROWS), bf16),
        in_specs=[VM] * 4 + [ANY], out_specs=VM,
        compiler_params=params(), cost_estimate=cost(1e5, 1.2e6), name="stack",
    )(mine, *ring, mine_half)
    rows = {t: second_axis(four, t) for t in (2, 1, 3)}

    other_four = swap(four)
    side = both_sides(whole)
    adj, adj2, degree = second_half(tile_mask, counts, *adjacency, other_four)

    total_shape = jax.ShapeDtypeStruct((ROWS, 192), f32)
    def product(kernel, kinds, pieces, *extra, after=(), name):
        return pl.pallas_call(
            functools.partial(kernel, kinds), out_shape=total_shape,
            in_specs=[VM] * (1 + len(extra) + len(pieces)) + [ANY] * len(after), out_specs=VM,
            compiler_params=params(), cost_estimate=blocks_cost(pieces), name=name,
        )(adj, *extra, *pieces, *after)

    total = product(product_first, ((0, 0), (0, 1)), [four, other_four], after=(side,), name="product_first")
    for t in (1, 2, 3):
        rows[t] = lax.optimization_barrier((total, rows[t]))[1]
    total = product(product_next, ((1, 0), (3, 0)), [rows[1], rows[3]], total, after=(near,), name="product_next")
    rows[2] = lax.optimization_barrier((total, rows[2]))[1]
    across = swap(rows[2])
    pieces = [swap(rows[1]), swap(rows[3]), rows[2]]
    total = product(product_next, ((1, 1), (3, 1), (2, 0)), pieces, total, name="product_more")
    pieces = [across]
    means = pl.pallas_call(
        functools.partial(product_last, ((2, 1),)), out_shape=[jax.ShapeDtypeStruct((SHARE, 192), bf16)] * NF,
        in_specs=[VM] * 4, out_specs=[VM] * NF,
        scratch_shapes=[pltpu.VMEM((ROWS, 192), f32)],
        compiler_params=params(), cost_estimate=blocks_cost(pieces), name="product_last",
    )(adj, total, degree, *pieces)

    side, near, means = lax.optimization_barrier((side, near, means))
    other_side, far = swap(side), swap(near)
    g = {0: means[0]} | {s: along_feat(means[s], s) for s in (2, 1, 3)}
    g = [g[s] for s in range(NF)]
    z_block = pl.pallas_call(
        hidden_kernel, out_shape=jax.ShapeDtypeStruct((TILE, TILE), bf16),
        in_specs=[VM] * 9, out_specs=VM,
        scratch_shapes=[pltpu.VMEM((SHARE, 512), f32)],
        compiler_params=params(), cost_estimate=cost(2 * 96 * 768 * 1024, 2e6), name="hidden",
    )(*g, whole, side, other_side, near, far)

    ring = {0: z_block} | {s: first_axis(z_block, s) for s in (2, 1, 3)}
    z_four = jnp.stack([ring[s] for s in SHIFTS])
    z_rows = {0: z_four} | {t: second_axis(z_four, t) for t in (2, 1, 3)}
    z_rows = [z_rows[t] for t in SHIFTS]
    z_pieces = [z for row in z_rows for z in (row, swap(row))]
    part = pl.pallas_call(
        scores_kernel, out_shape=jax.ShapeDtypeStruct((160, ROWS), bf16),
        in_specs=[VM] * 10, out_specs=VM,
        scratch_shapes=[pltpu.VMEM((NV * TILE, 256), bf16)],
        compiler_params=params(), cost_estimate=cost(2 * 384 * 4096 * 256, 5e6), name="scores",
    )(adj2, degree, *z_pieces)
    parts = {0: part} | {s: along_feat(part, s) for s in (2, 1, 3)}
    parts = [parts[s] for s in range(NF)]
    return pl.pallas_call(
        sum_kernel, out_shape=jax.ShapeDtypeStruct((CLS, ROWS), f32),
        in_specs=[VM] * 5, out_specs=VM,
        compiler_params=params(), cost_estimate=cost(3e5, 8e5), name="sum",
    )(*parts, jnp.pad(b_out, (0, 256 - CLS)).reshape(1, 256)).T


def solution(mesh):
    placed = (
        P("vert", "feat"),
        P("vert", None),
        P("vert", None),
        P("feat", None),
        P("feat"),
        P("feat", None),
        P(),
    )
    return jax.shard_map(
        local, mesh=mesh, in_specs=placed, out_specs=P("vert", None), check_vma=False
    )
```

```python
import functools

import jax
import jax.numpy as jnp
from jax import lax
from jax.experimental import pallas as pl
from jax.experimental.pallas import tpu as pltpu
from jax.sharding import PartitionSpec as P

TILE = 128
ROWS = 384
NV = 32
NF = 4
SHARE = ROWS // NF
CLS = 153
bf16 = jnp.bfloat16
f32 = jnp.float32
NT = (((1,), (1,)), ((), ()))
VM = pl.BlockSpec(memory_space=pltpu.VMEM)
SM = pl.BlockSpec(memory_space=pltpu.SMEM)
HB = pl.BlockSpec(memory_space=pltpu.HBM)
ANY = pl.BlockSpec(memory_space=pl.ANY)


def here():
    return lax.axis_index("vert").astype(jnp.int32), lax.axis_index("feat").astype(jnp.int32)


def source(me, s, t, c):
    spot = lax.div(me, 2)
    x, z = lax.div(spot, NF), lax.rem(spot, NF)
    x = lax.rem(x + NF - jnp.where(c == 0, s, t), NF)
    z = lax.rem(z + NF - jnp.where(c == 0, t, s), NF)
    return (x * NF + z) * 2 + c


SHIFTS = (0, 2, 1, 3)


def params(mib=16):
    return pltpu.CompilerParams(vmem_limit_bytes=mib * 2**20)


def cost(flops, nbytes):
    return pl.CostEstimate(flops=int(flops), bytes_accessed=int(nbytes), transcendentals=0)


def positions(move):
    pairs = []
    for x in range(4):
        for z in range(4):
            for c in range(2):
                xx, zz, cc = move(x, z, c)
                pairs.append(((x * 4 + z) * 2 + c, (xx % 4 * 4 + zz % 4) * 2 + cc % 2))
    return pairs


def first_axis(value, shift):
    return lax.ppermute(value, "vert", positions(lambda x, z, c: (x + shift * (1 - c), z + shift * c, c)))


def second_axis(value, shift):
    return lax.ppermute(value, "vert", positions(lambda x, z, c: (x + shift * c, z + shift * (1 - c), c)))


def swap(value):
    return lax.ppermute(value, "vert", positions(lambda x, z, c: (x, z, 1 - c)))


def along_feat(value, shift):
    return lax.ppermute(value, "feat", [(i, (i + shift) % NF) for i in range(NF)])


def both_sides(value):
    pairs = [(f * NV + v, (f + 1 - 2 * (v % 2)) % NF * NV + v) for v in range(NV) for f in range(NF)]
    return lax.ppermute(value, ("feat", "vert"), pairs)


CHUNK = 4 * ROWS
STEPS = NV * ROWS // CHUNK
SLOTS = 3
SPLIT = 3


def adjacency_kernel(part, mask, counts, *refs):
    if part == 0:
        w_in, w_out_t, b_in, adj, adj2, degree, whole, mine, slots, sems, mask_sm, one, w1, w2, b1, three = refs
        extra = [(w_in, w1), (w_out_t, w2), (b_in, b1)]
    else:
        adj, adj2, degree, slots, sems, mask_sm, one = refs[4:]
        extra = []
    me, feat = here()
    first, last = (0, SPLIT) if part == 0 else (SPLIT, STEPS)
    mask_copy = pltpu.make_async_copy(mask, mask_sm, one)
    mask_copy.start()
    source_row = lax.broadcasted_iota(jnp.int32, (ROWS, TILE), 0)
    target = lax.broadcasted_iota(jnp.int32, (ROWS, TILE), 1)
    chosen = (source_row == target + feat * SHARE) & (target < SHARE)
    pick = (chosen | (target == SHARE)).astype(f32).astype(bf16)
    inside = lax.broadcasted_iota(jnp.int32, (TILE, TILE), 1) < SHARE

    def fetch(step, slot):
        start = pl.multiple_of(step * CHUNK, CHUNK)
        return pltpu.make_async_copy(counts.at[:, pl.ds(start, CHUNK)], slots.at[slot], sems.at[slot])

    for i in range(SLOTS - 1):
        fetch(first + i, i).start()
    extra = [pltpu.make_async_copy(a, b, three.at[i]) for i, (a, b) in enumerate(extra)]
    for copy in extra:
        copy.start()
    if part == 0:
        degree[...] = jnp.zeros_like(degree)
    mask_copy.wait()

    @pl.loop(first, last)
    def _(step):
        slot = lax.rem(step - first, SLOTS)

        @pl.when(step + SLOTS - 1 < last)
        def _():
            fetch(step + SLOTS - 1, lax.rem(step - first + SLOTS - 1, SLOTS)).start()

        fetch(step, slot).wait()
        for j in range(CHUNK // ROWS):
            base = pl.multiple_of(step * CHUNK + j * ROWS, ROWS)
            place = pl.multiple_of((step * (CHUNK // ROWS) + j) * TILE, TILE)
            for i in range(ROWS // TILE):
                rows = slice(i * TILE, (i + 1) * TILE)
                strip = []
                for k in range(ROWS // TILE):
                    stored = mask_sm[i, (step * (CHUNK // ROWS) + j) * (ROWS // TILE) + k].astype(f32)
                    tile = slots[slot, rows, j * ROWS + k * TILE : j * ROWS + (k + 1) * TILE]
                    strip.append((tile.astype(f32) * stored).astype(bf16))
                strip = jnp.concatenate(strip, axis=1)
                adj[rows, pl.ds(base, ROWS)] = strip
                part = jnp.dot(strip, pick, preferred_element_type=f32)
                degree[rows, :] += part
                adj2[rows, pl.ds(place, TILE)] = jnp.where(inside, part, 0.0).astype(bf16)

    for copy in extra:
        copy.wait()
    if part == 0:
        pack(w1, w2, b1, whole, mine)
        return
    place = pl.ds(pl.multiple_of(me * TILE, TILE), TILE)
    adj2[:, place] = (adj2[:, place].astype(f32) + chosen.astype(f32)).astype(bf16)
    row = lax.broadcasted_iota(jnp.int32, (ROWS, ROWS), 0)
    col = lax.broadcasted_iota(jnp.int32, (ROWS, ROWS), 1)
    place = pl.ds(pl.multiple_of(me * ROWS, ROWS), ROWS)
    adj[:, place] = (adj[:, place].astype(f32) + (row == col).astype(f32)).astype(bf16)
    degree[...] = jnp.broadcast_to(1.0 / (degree[:, SHARE : SHARE + 1] + 1.0), degree.shape)


ADJACENCY = [
    pltpu.VMEM((ROWS, NV * ROWS), bf16),
    pltpu.VMEM((ROWS, NV * TILE), bf16),
    pltpu.VMEM((ROWS, TILE), f32),
]
ADJACENCY_SCRATCH = [
    pltpu.VMEM((SLOTS, ROWS, CHUNK), jnp.int32),
    pltpu.SemaphoreType.DMA((SLOTS,)),
    pltpu.SMEM((ROWS // TILE, NV * ROWS // TILE), jnp.int32),
    pltpu.SemaphoreType.DMA(()),
]


def first_half(tile_mask, counts, w_in, w_out_t, b_in):
    return pl.pallas_call(
        functools.partial(adjacency_kernel, 0),
        in_specs=[HB] * 5,
        out_specs=[VM] * 5,
        out_shape=ADJACENCY + [
            jax.ShapeDtypeStruct((2, 256, 512), bf16),
            jax.ShapeDtypeStruct((256, 512), bf16),
        ],
        scratch_shapes=ADJACENCY_SCRATCH + [
            pltpu.VMEM((192, 1024), bf16),
            pltpu.VMEM((CLS, 256), bf16),
            pltpu.VMEM((1, 256), f32),
            pltpu.SemaphoreType.DMA((3,)),
        ],
        compiler_params=params(24),
        cost_estimate=cost(1.2e9, 16e6),
        name="adjacency_first",
    )(tile_mask, counts, w_in, w_out_t, b_in)


def second_half(tile_mask, counts, adj, adj2, degree, after):
    return pl.pallas_call(
        functools.partial(adjacency_kernel, 1),
        in_specs=[HB] * 2 + [VM] * 3 + [ANY],
        out_specs=[VM] * 3,
        out_shape=ADJACENCY,
        input_output_aliases={2: 0, 3: 1, 4: 2},
        scratch_shapes=ADJACENCY_SCRATCH,
        compiler_params=params(24),
        cost_estimate=cost(1.2e9, 16e6),
        name="adjacency_second",
    )(tile_mask, counts, adj, adj2, degree, after)


def pack(w_in, w_out_t, b_in, whole, mine):
    zero = jnp.zeros((192 - CLS, TILE), f32)
    for half in range(2):
        lanes = slice(TILE * half, TILE * (half + 1))
        for k in range(NF):
            whole[half, 0:192, k * TILE : (k + 1) * TILE] = w_in[:, 256 * k + TILE * half : 256 * k + TILE * (half + 1)]
        w = jnp.concatenate([w_out_t[:, lanes].astype(f32), zero], axis=0)
        for k in range(NF):
            whole[half, 192:240, k * TILE : (k + 1) * TILE] = w[48 * k : 48 * (k + 1)].astype(bf16)
        b = jnp.broadcast_to(b_in[:, lanes], (16, TILE))
        hi = b.astype(bf16).astype(f32)
        mid = (b - hi).astype(bf16).astype(f32)
        low = b - hi - mid
        row = lax.broadcasted_iota(jnp.int32, (16, TILE), 0)
        b = jnp.where(row == 0, hi, jnp.where(row == 1, mid, jnp.where(row == 2, low, 0.0)))
        whole[half, 240:256, 0:TILE] = b.astype(bf16)
        whole[half, 240:256, TILE:] = jnp.zeros((16, 512 - TILE), bf16)
    mine[...] = whole[lax.rem(here()[0], 2)]


def stack_kernel(a, b, c, d, after, out):
    for i, part in enumerate((a, b, c, d)):
        out[i] = part[...]


def add_blocks(kinds, adj, total, pieces):
    me, _ = here()
    for (shift, p), piece in zip(kinds, pieces, strict=True):
        core = lax.rem(me + p, 2)
        for b in range(NF):
            src = source(me, SHIFTS[b], shift, core)
            src = pl.multiple_of(src * ROWS, ROWS)
            total = total + lax.dot_general(adj[:, pl.ds(src, ROWS)], piece[b], NT, preferred_element_type=f32)
    return total


def product_first(kinds, adj, *refs):
    refs[-1][...] = add_blocks(kinds, adj, jnp.zeros(refs[-1].shape, f32), refs[: len(kinds)])


def product_next(kinds, adj, before, *refs):
    refs[-1][...] = add_blocks(kinds, adj, before[...], refs[: len(kinds)])


def product_last(kinds, adj, before, degree, *refs):
    pieces, outs, mean = refs[:-5], refs[-5:-1], refs[-1]
    feat = here()[1]
    total = add_blocks(kinds, adj, before[...], pieces)
    mean[...] = total * degree[:, :1]
    for s in range(NF):
        q = lax.rem(feat + s, NF)
        outs[s][...] = mean[pl.ds(pl.multiple_of(q * SHARE, SHARE), SHARE), :].astype(bf16)


def blocks_cost(pieces):
    n = sum(p.shape[0] for p in pieces)
    return cost(2 * 384 * 384 * 256 * n, n * 450e3)


def hidden_kernel(g0, g1, g2, g3, own, side, other_side, near, far, z_out, hid):
    me, feat = here()
    core = lax.rem(me, 2)
    even = core == 0
    ga = jnp.where(even, g1[...].astype(f32), g3[...].astype(f32)).astype(bf16)
    gb = jnp.where(even, g3[...].astype(f32), g1[...].astype(f32)).astype(bf16)
    down, up = lax.rem(feat + NF - 1, NF), lax.rem(feat + 1, NF)
    across = lax.rem(feat + 2, NF)
    total = jnp.zeros((SHARE, 192), f32)
    for half, opposite in ((core, near), (1 - core, far)):
        parts = (
            (g0[...], own.at[half], feat),
            (ga, side.at[half], jnp.where(even, down, up)),
            (gb, other_side.at[half], jnp.where(even, up, down)),
            (g2[...], opposite, across),
        )
        pre = jnp.zeros((SHARE, 512), f32)
        for g, part, _ in parts:
            pre = pre + jnp.dot(g, part[0:192, :], preferred_element_type=f32)
        hid[...] = pre
        for _, part, owner in parts:
            lanes = pl.ds(pl.multiple_of(owner * TILE, TILE), TILE)
            b = part[240:256, 0:TILE].astype(f32)
            bias = b[0:1] + b[1:2] + b[2:3]
            unit = jnp.maximum(hid[:, lanes] + bias, 0.0).astype(bf16)
            w = part[192:240, :]
            w = jnp.concatenate([w[:, k * TILE : (k + 1) * TILE] for k in range(NF)], axis=0)
            total = total + lax.dot_general(unit, w, NT, preferred_element_type=f32)
    z_out[0:SHARE, :] = total[:, :TILE].astype(bf16)
    tail = total[:, TILE : TILE + 32]
    packed = jnp.concatenate([tail[0:32], tail[32:64], tail[64:96], jnp.zeros((32, 32), f32)], axis=1)
    z_out[SHARE:, :] = packed.astype(bf16)


def unpack(kinds, pieces, z_all):
    me, _ = here()
    for (shift, p), piece in zip(kinds, pieces, strict=True):
        for b in range(NF):
            src = source(me, SHIFTS[b], shift, lax.rem(me + p, 2))
            src = pl.multiple_of(src * TILE, TILE)
            z_all[pl.ds(src, TILE), :TILE] = piece[b]
            tail = piece[b, SHARE:, :].astype(f32)
            tail = jnp.concatenate([tail[:, 0:32], tail[:, 32:64], tail[:, 64:96], jnp.zeros((32, 32), f32)], axis=0)
            tail = jnp.concatenate([tail, jnp.zeros((TILE, 96), f32)], axis=1)
            z_all[pl.ds(src, TILE), TILE:] = tail.astype(bf16)


def unpack_kernel(kinds, *refs):
    unpack(kinds, refs[: len(kinds)], refs[-1])


def scores_kernel(kinds, adj2, inverse, before, *refs):
    out, z_all = refs[-2], refs[-1]
    unpack(kinds, refs[: len(kinds)], z_all)
    part = jnp.dot(adj2[...], z_all[...], preferred_element_type=f32) * inverse[:, :1]
    out[...] = part.T[0:160].astype(bf16)


def sum_kernel(p0, p1, p2, p3, b_out, out):
    total = (p0[...].astype(f32) + p2[...].astype(f32)) + (p1[...].astype(f32) + p3[...].astype(f32))
    bias = jnp.broadcast_to(b_out[...], (TILE, 256)).T[:, 0:1]
    out[...] = total[0:CLS] + bias[0:CLS]


def local(features, counts, tile_mask, w_in, b_in, w_out, b_out):
    tile_mask, counts, *weights = (
        pltpu.with_memory_space_constraint(a, pltpu.HBM)
        for a in (tile_mask, counts, w_in, w_out.T, b_in.reshape(1, 256))
    )
    *adjacency, whole, mine_half = first_half(tile_mask, counts, *weights)
    near = along_feat(mine_half, 2)

    mine = features.T
    ring = [first_axis(mine, s) for s in (2, 1, 3)]
    four = pl.pallas_call(
        stack_kernel, out_shape=jax.ShapeDtypeStruct((NF, 192, ROWS), bf16),
        in_specs=[VM] * 4 + [ANY], out_specs=VM,
        compiler_params=params(), cost_estimate=cost(1e5, 1.2e6), name="stack",
    )(mine, *ring, mine_half)
    rows = {t: second_axis(four, t) for t in (2, 1, 3)}

    other_four = swap(four)
    side = both_sides(whole)
    adj, adj2, degree = second_half(tile_mask, counts, *adjacency, other_four)

    total_shape = jax.ShapeDtypeStruct((ROWS, 192), f32)
    def product(kernel, kinds, pieces, *extra, after=(), name):
        return pl.pallas_call(
            functools.partial(kernel, kinds), out_shape=total_shape,
            in_specs=[VM] * (1 + len(extra) + len(pieces)) + [ANY] * len(after), out_specs=VM,
            compiler_params=params(), cost_estimate=blocks_cost(pieces), name=name,
        )(adj, *extra, *pieces, *after)

    total = product(product_first, ((0, 0), (0, 1)), [four, other_four], after=(side,), name="product_first")
    for t in (1, 2, 3):
        rows[t] = lax.optimization_barrier((total, rows[t]))[1]
    total = product(product_next, ((1, 0), (3, 0)), [rows[1], rows[3]], total, after=(near,), name="product_next")
    rows[2] = lax.optimization_barrier((total, rows[2]))[1]
    across = swap(rows[2])
    pieces = [swap(rows[1]), swap(rows[3]), rows[2]]
    total = product(product_next, ((1, 1), (3, 1), (2, 0)), pieces, total, name="product_more")
    pieces = [across]
    means = pl.pallas_call(
        functools.partial(product_last, ((2, 1),)), out_shape=[jax.ShapeDtypeStruct((SHARE, 192), bf16)] * NF,
        in_specs=[VM] * 4, out_specs=[VM] * NF,
        scratch_shapes=[pltpu.VMEM((ROWS, 192), f32)],
        compiler_params=params(), cost_estimate=blocks_cost(pieces), name="product_last",
    )(adj, total, degree, *pieces)

    side, near, means = lax.optimization_barrier((side, near, means))
    other_side, far = swap(side), swap(near)
    g = {0: means[0]} | {s: along_feat(means[s], s) for s in (2, 1, 3)}
    g = [g[s] for s in range(NF)]
    z_block = pl.pallas_call(
        hidden_kernel, out_shape=jax.ShapeDtypeStruct((TILE, TILE), bf16),
        in_specs=[VM] * 9, out_specs=VM,
        scratch_shapes=[pltpu.VMEM((SHARE, 512), f32)],
        compiler_params=params(), cost_estimate=cost(2 * 96 * 768 * 1024, 2e6), name="hidden",
    )(*g, whole, side, other_side, near, far)

    ring = {0: z_block} | {s: first_axis(z_block, s) for s in (2, 1, 3)}
    z_four = jnp.stack([ring[s] for s in SHIFTS])
    z_rows = {0: z_four} | {t: second_axis(z_four, t) for t in (2, 1, 3)}
    z_rows = [z_rows[t] for t in SHIFTS]
    z_rows = dict(zip(SHIFTS, z_rows, strict=True))
    z_other = {t: swap(z_rows[t]) for t in SHIFTS}
    z_shape = pltpu.VMEM((NV * TILE, 256), bf16)
    early = ((0, 0), (0, 1), (2, 0), (1, 0), (3, 0))
    late = ((2, 1), (1, 1), (3, 1))
    z_all = pl.pallas_call(
        functools.partial(unpack_kernel, early), out_shape=z_shape,
        in_specs=[VM] * len(early), out_specs=VM,
        compiler_params=params(), cost_estimate=cost(1e5, 2e6), name="unpack",
    )(*((z_rows, z_other)[p][t] for t, p in early))
    part, _ = pl.pallas_call(
        functools.partial(scores_kernel, late),
        out_shape=[jax.ShapeDtypeStruct((160, ROWS), bf16), z_shape],
        in_specs=[VM] * (3 + len(late)), out_specs=[VM] * 2, input_output_aliases={2: 1},
        compiler_params=params(), cost_estimate=cost(2 * 384 * 4096 * 256, 5e6), name="scores",
    )(adj2, degree, z_all, *((z_rows, z_other)[p][t] for t, p in late))
    parts = {0: part} | {s: along_feat(part, s) for s in (2, 1, 3)}
    parts = [parts[s] for s in range(NF)]
    return pl.pallas_call(
        sum_kernel, out_shape=jax.ShapeDtypeStruct((CLS, ROWS), f32),
        in_specs=[VM] * 5, out_specs=VM,
        compiler_params=params(), cost_estimate=cost(3e5, 8e5), name="sum",
    )(*parts, jnp.pad(b_out, (0, 256 - CLS)).reshape(1, 256)).T


def solution(mesh):
    placed = (
        P("vert", "feat"),
        P("vert", None),
        P("vert", None),
        P("feat", None),
        P("feat"),
        P("feat", None),
        P(),
    )
    return jax.shard_map(
        local, mesh=mesh, in_specs=placed, out_specs=P("vert", None), check_vma=False
    )
```

```python
import functools

import jax
import jax.numpy as jnp
from jax import lax
from jax.experimental import pallas as pl
from jax.experimental.pallas import tpu as pltpu
from jax.sharding import PartitionSpec as P

TILE = 128
ROWS = 384
NV = 32
NF = 4
SHARE = ROWS // NF
CLS = 153
bf16 = jnp.bfloat16
f32 = jnp.float32
NT = (((1,), (1,)), ((), ()))
VM = pl.BlockSpec(memory_space=pltpu.VMEM)
SM = pl.BlockSpec(memory_space=pltpu.SMEM)
HB = pl.BlockSpec(memory_space=pltpu.HBM)
ANY = pl.BlockSpec(memory_space=pl.ANY)


def here():
    return lax.axis_index("vert").astype(jnp.int32), lax.axis_index("feat").astype(jnp.int32)


def source(me, s, t, c):
    spot = lax.div(me, 2)
    x, z = lax.div(spot, NF), lax.rem(spot, NF)
    x = lax.rem(x + NF - jnp.where(c == 0, s, t), NF)
    z = lax.rem(z + NF - jnp.where(c == 0, t, s), NF)
    return (x * NF + z) * 2 + c


SHIFTS = (0, 2, 1, 3)


def params(mib=16):
    return pltpu.CompilerParams(vmem_limit_bytes=mib * 2**20)


def cost(flops, nbytes):
    return pl.CostEstimate(flops=int(flops), bytes_accessed=int(nbytes), transcendentals=0)


def positions(move):
    pairs = []
    for x in range(4):
        for z in range(4):
            for c in range(2):
                xx, zz, cc = move(x, z, c)
                pairs.append(((x * 4 + z) * 2 + c, (xx % 4 * 4 + zz % 4) * 2 + cc % 2))
    return pairs


def first_axis(value, shift):
    return lax.ppermute(value, "vert", positions(lambda x, z, c: (x + shift * (1 - c), z + shift * c, c)))


def second_axis(value, shift):
    return lax.ppermute(value, "vert", positions(lambda x, z, c: (x + shift * c, z + shift * (1 - c), c)))


def swap(value):
    return lax.ppermute(value, "vert", positions(lambda x, z, c: (x, z, 1 - c)))


def along_feat(value, shift):
    return lax.ppermute(value, "feat", [(i, (i + shift) % NF) for i in range(NF)])


def both_sides(value):
    pairs = [(f * NV + v, (f + 1 - 2 * (v % 2)) % NF * NV + v) for v in range(NV) for f in range(NF)]
    return lax.ppermute(value, ("feat", "vert"), pairs)


CHUNK = 4 * ROWS
STEPS = NV * ROWS // CHUNK
SLOTS = 3
SPLIT = 3


def adjacency_kernel(part, mask, counts, *refs):
    if part == 0:
        w_in, w_out_t, b_in, adj, adj2, degree, whole, mine, slots, sems, mask_sm, one, w1, w2, b1, three = refs
        extra = [(w_in, w1), (w_out_t, w2), (b_in, b1)]
    else:
        adj, adj2, degree, slots, sems, mask_sm, one = refs[4:]
        extra = []
    me, feat = here()
    first, last = (0, SPLIT) if part == 0 else (SPLIT, STEPS)
    mask_copy = pltpu.make_async_copy(mask, mask_sm, one)
    mask_copy.start()
    source_row = lax.broadcasted_iota(jnp.int32, (ROWS, TILE), 0)
    target = lax.broadcasted_iota(jnp.int32, (ROWS, TILE), 1)
    chosen = (source_row == target + feat * SHARE) & (target < SHARE)
    pick = (chosen | (target == SHARE)).astype(f32).astype(bf16)
    inside = lax.broadcasted_iota(jnp.int32, (TILE, TILE), 1) < SHARE

    def fetch(step, slot):
        start = pl.multiple_of(step * CHUNK, CHUNK)
        return pltpu.make_async_copy(counts.at[:, pl.ds(start, CHUNK)], slots.at[slot], sems.at[slot])

    for i in range(SLOTS - 1):
        fetch(first + i, i).start()
    extra = [pltpu.make_async_copy(a, b, three.at[i]) for i, (a, b) in enumerate(extra)]
    for copy in extra:
        copy.start()
    if part == 0:
        degree[...] = jnp.zeros_like(degree)
    mask_copy.wait()

    @pl.loop(first, last)
    def _(step):
        slot = lax.rem(step - first, SLOTS)

        @pl.when(step + SLOTS - 1 < last)
        def _():
            fetch(step + SLOTS - 1, lax.rem(step - first + SLOTS - 1, SLOTS)).start()

        fetch(step, slot).wait()
        for j in range(CHUNK // ROWS):
            base = pl.multiple_of(step * CHUNK + j * ROWS, ROWS)
            place = pl.multiple_of((step * (CHUNK // ROWS) + j) * TILE, TILE)
            for i in range(ROWS // TILE):
                rows = slice(i * TILE, (i + 1) * TILE)
                strip = []
                for k in range(ROWS // TILE):
                    stored = mask_sm[i, (step * (CHUNK // ROWS) + j) * (ROWS // TILE) + k].astype(f32)
                    tile = slots[slot, rows, j * ROWS + k * TILE : j * ROWS + (k + 1) * TILE]
                    strip.append((tile.astype(f32) * stored).astype(bf16))
                strip = jnp.concatenate(strip, axis=1)
                adj[rows, pl.ds(base, ROWS)] = strip
                part = jnp.dot(strip, pick, preferred_element_type=f32)
                degree[rows, :] += part
                adj2[rows, pl.ds(place, TILE)] = jnp.where(inside, part, 0.0).astype(bf16)

    for copy in extra:
        copy.wait()
    if part == 0:
        pack(w1, w2, b1, whole, mine)
        return
    place = pl.ds(pl.multiple_of(me * TILE, TILE), TILE)
    adj2[:, place] = (adj2[:, place].astype(f32) + chosen.astype(f32)).astype(bf16)
    row = lax.broadcasted_iota(jnp.int32, (ROWS, ROWS), 0)
    col = lax.broadcasted_iota(jnp.int32, (ROWS, ROWS), 1)
    place = pl.ds(pl.multiple_of(me * ROWS, ROWS), ROWS)
    adj[:, place] = (adj[:, place].astype(f32) + (row == col).astype(f32)).astype(bf16)
    degree[...] = jnp.broadcast_to(1.0 / (degree[:, SHARE : SHARE + 1] + 1.0), degree.shape)


ADJACENCY = [
    pltpu.VMEM((ROWS, NV * ROWS), bf16),
    pltpu.VMEM((ROWS, NV * TILE), bf16),
    pltpu.VMEM((ROWS, TILE), f32),
]
ADJACENCY_SCRATCH = [
    pltpu.VMEM((SLOTS, ROWS, CHUNK), jnp.int32),
    pltpu.SemaphoreType.DMA((SLOTS,)),
    pltpu.SMEM((ROWS // TILE, NV * ROWS // TILE), jnp.int32),
    pltpu.SemaphoreType.DMA(()),
]


def first_half(tile_mask, counts, w_in, w_out_t, b_in):
    return pl.pallas_call(
        functools.partial(adjacency_kernel, 0),
        in_specs=[HB] * 5,
        out_specs=[VM] * 5,
        out_shape=ADJACENCY + [
            jax.ShapeDtypeStruct((2, 256, 512), bf16),
            jax.ShapeDtypeStruct((256, 512), bf16),
        ],
        scratch_shapes=ADJACENCY_SCRATCH + [
            pltpu.VMEM((192, 1024), bf16),
            pltpu.VMEM((CLS, 256), bf16),
            pltpu.VMEM((1, 256), f32),
            pltpu.SemaphoreType.DMA((3,)),
        ],
        compiler_params=params(24),
        cost_estimate=cost(1.2e9, 16e6),
        name="adjacency_first",
    )(tile_mask, counts, w_in, w_out_t, b_in)


def second_half(tile_mask, counts, adj, adj2, degree, after):
    return pl.pallas_call(
        functools.partial(adjacency_kernel, 1),
        in_specs=[HB] * 2 + [VM] * 3 + [ANY],
        out_specs=[VM] * 3,
        out_shape=ADJACENCY,
        input_output_aliases={2: 0, 3: 1, 4: 2},
        scratch_shapes=ADJACENCY_SCRATCH,
        compiler_params=params(24),
        cost_estimate=cost(1.2e9, 16e6),
        name="adjacency_second",
    )(tile_mask, counts, adj, adj2, degree, after)


def pack(w_in, w_out_t, b_in, whole, mine):
    zero = jnp.zeros((192 - CLS, TILE), f32)
    for half in range(2):
        lanes = slice(TILE * half, TILE * (half + 1))
        for k in range(NF):
            whole[half, 0:192, k * TILE : (k + 1) * TILE] = w_in[:, 256 * k + TILE * half : 256 * k + TILE * (half + 1)]
        w = jnp.concatenate([w_out_t[:, lanes].astype(f32), zero], axis=0)
        for k in range(NF):
            whole[half, 192:240, k * TILE : (k + 1) * TILE] = w[48 * k : 48 * (k + 1)].astype(bf16)
        b = jnp.broadcast_to(b_in[:, lanes], (16, TILE))
        hi = b.astype(bf16).astype(f32)
        mid = (b - hi).astype(bf16).astype(f32)
        low = b - hi - mid
        row = lax.broadcasted_iota(jnp.int32, (16, TILE), 0)
        b = jnp.where(row == 0, hi, jnp.where(row == 1, mid, jnp.where(row == 2, low, 0.0)))
        whole[half, 240:256, 0:TILE] = b.astype(bf16)
        whole[half, 240:256, TILE:] = jnp.zeros((16, 512 - TILE), bf16)
    mine[...] = whole[lax.rem(here()[0], 2)]


def stack_kernel(a, b, c, d, after, out):
    for i, part in enumerate((a, b, c, d)):
        out[i] = part[...]


def add_blocks(kinds, adj, total, pieces):
    me, _ = here()
    for (shift, p), piece in zip(kinds, pieces, strict=True):
        core = lax.rem(me + p, 2)
        for b in range(NF):
            src = source(me, SHIFTS[b], shift, core)
            src = pl.multiple_of(src * ROWS, ROWS)
            total = total + lax.dot_general(adj[:, pl.ds(src, ROWS)], piece[b], NT, preferred_element_type=f32)
    return total


def product_first(kinds, adj, *refs):
    refs[-1][...] = add_blocks(kinds, adj, jnp.zeros(refs[-1].shape, f32), refs[: len(kinds)])


def product_next(kinds, adj, before, *refs):
    refs[-1][...] = add_blocks(kinds, adj, before[...], refs[: len(kinds)])


def product_last(kinds, adj, before, degree, *refs):
    pieces, outs, mean = refs[: len(kinds)], refs[-5:-1], refs[-1]
    feat = here()[1]
    total = add_blocks(kinds, adj, before[...], pieces)
    mean[...] = total * degree[:, :1]
    for s in range(NF):
        q = lax.rem(feat + s, NF)
        outs[s][...] = mean[pl.ds(pl.multiple_of(q * SHARE, SHARE), SHARE), :].astype(bf16)


def blocks_cost(pieces):
    n = sum(p.shape[0] for p in pieces)
    return cost(2 * 384 * 384 * 256 * n, n * 450e3)


def hidden_kernel(g0, g1, g2, g3, own, side, other_side, near, far, z_out, hid):
    me, feat = here()
    core = lax.rem(me, 2)
    even = core == 0
    ga = jnp.where(even, g1[...].astype(f32), g3[...].astype(f32)).astype(bf16)
    gb = jnp.where(even, g3[...].astype(f32), g1[...].astype(f32)).astype(bf16)
    down, up = lax.rem(feat + NF - 1, NF), lax.rem(feat + 1, NF)
    across = lax.rem(feat + 2, NF)
    total = jnp.zeros((SHARE, 192), f32)
    for half, opposite in ((core, near), (1 - core, far)):
        parts = (
            (g0[...], own.at[half], feat),
            (ga, side.at[half], jnp.where(even, down, up)),
            (gb, other_side.at[half], jnp.where(even, up, down)),
            (g2[...], opposite, across),
        )
        pre = jnp.zeros((SHARE, 512), f32)
        for g, part, _ in parts:
            pre = pre + jnp.dot(g, part[0:192, :], preferred_element_type=f32)
        hid[...] = pre
        for _, part, owner in parts:
            lanes = pl.ds(pl.multiple_of(owner * TILE, TILE), TILE)
            b = part[240:256, 0:TILE].astype(f32)
            bias = b[0:1] + b[1:2] + b[2:3]
            unit = jnp.maximum(hid[:, lanes] + bias, 0.0).astype(bf16)
            w = part[192:240, :]
            w = jnp.concatenate([w[:, k * TILE : (k + 1) * TILE] for k in range(NF)], axis=0)
            total = total + lax.dot_general(unit, w, NT, preferred_element_type=f32)
    z_out[0:SHARE, :] = total[:, :TILE].astype(bf16)
    tail = total[:, TILE : TILE + 32]
    packed = jnp.concatenate([tail[0:32], tail[32:64], tail[64:96], jnp.zeros((32, 32), f32)], axis=1)
    z_out[SHARE:, :] = packed.astype(bf16)


def unpack(kinds, pieces, z_all):
    me, _ = here()
    for (shift, p), piece in zip(kinds, pieces, strict=True):
        for b in range(NF):
            src = source(me, SHIFTS[b], shift, lax.rem(me + p, 2))
            src = pl.multiple_of(src * TILE, TILE)
            z_all[pl.ds(src, TILE), :TILE] = piece[b]
            tail = piece[b, SHARE:, :].astype(f32)
            tail = jnp.concatenate([tail[:, 0:32], tail[:, 32:64], tail[:, 64:96], jnp.zeros((32, 32), f32)], axis=0)
            tail = jnp.concatenate([tail, jnp.zeros((TILE, 96), f32)], axis=1)
            z_all[pl.ds(src, TILE), TILE:] = tail.astype(bf16)


def unpack_kernel(kinds, *refs):
    unpack(kinds, refs[: len(kinds)], refs[-1])


def scores_kernel(kinds, adj2, inverse, before, *refs):
    out, z_all = refs[-2], refs[-1]
    unpack(kinds, refs[: len(kinds)], z_all)
    part = jnp.dot(adj2[...], z_all[...], preferred_element_type=f32) * inverse[:, :1]
    out[...] = part.T[0:160].astype(bf16)


def sum_kernel(p0, p1, p2, p3, b_out, out):
    total = (p0[...].astype(f32) + p2[...].astype(f32)) + (p1[...].astype(f32) + p3[...].astype(f32))
    bias = jnp.broadcast_to(b_out[...], (TILE, 256)).T[:, 0:1]
    out[...] = total[0:CLS] + bias[0:CLS]


def local(features, counts, tile_mask, w_in, b_in, w_out, b_out):
    tile_mask, counts, *weights = (
        pltpu.with_memory_space_constraint(a, pltpu.HBM)
        for a in (tile_mask, counts, w_in, w_out.T, b_in.reshape(1, 256))
    )
    *adjacency, whole, mine_half = first_half(tile_mask, counts, *weights)
    near = along_feat(mine_half, 2)

    mine = features.T
    ring = [first_axis(mine, s) for s in (2, 1, 3)]
    four = pl.pallas_call(
        stack_kernel, out_shape=jax.ShapeDtypeStruct((NF, 192, ROWS), bf16),
        in_specs=[VM] * 4 + [ANY], out_specs=VM,
        compiler_params=params(), cost_estimate=cost(1e5, 1.2e6), name="stack",
    )(mine, *ring, mine_half)
    rows = {t: second_axis(four, t) for t in (2, 1, 3)}

    other_four = swap(four)
    side = both_sides(whole)
    adj, adj2, degree = second_half(tile_mask, counts, *adjacency, other_four)

    total_shape = jax.ShapeDtypeStruct((ROWS, 192), f32)
    def product(kernel, kinds, pieces, *extra, after=(), name):
        return pl.pallas_call(
            functools.partial(kernel, kinds), out_shape=total_shape,
            in_specs=[VM] * (1 + len(extra) + len(pieces)) + [ANY] * len(after), out_specs=VM,
            compiler_params=params(), cost_estimate=blocks_cost(pieces), name=name,
        )(adj, *extra, *pieces, *after)

    total = product(product_first, ((0, 0), (0, 1)), [four, other_four], after=(side,), name="product_first")
    for t in (1, 2, 3):
        rows[t] = lax.optimization_barrier((total, rows[t]))[1]
    total = product(product_next, ((1, 0), (3, 0)), [rows[1], rows[3]], total, after=(near,), name="product_next")
    rows[2] = lax.optimization_barrier((total, rows[2]))[1]
    other_side = swap(lax.optimization_barrier((side, total))[0])
    far = swap(lax.optimization_barrier((near, total))[0])
    across = swap(rows[2])
    pieces = [swap(rows[1]), swap(rows[3]), rows[2]]
    total = product(product_next, ((1, 1), (3, 1), (2, 0)), pieces, total, name="product_more")
    pieces = [across]
    means = pl.pallas_call(
        functools.partial(product_last, ((2, 1),)), out_shape=[jax.ShapeDtypeStruct((SHARE, 192), bf16)] * NF,
        in_specs=[VM] * 4 + [ANY] * 2, out_specs=[VM] * NF,
        scratch_shapes=[pltpu.VMEM((ROWS, 192), f32)],
        compiler_params=params(), cost_estimate=blocks_cost(pieces), name="product_last",
    )(adj, total, degree, *pieces, other_side, far)

    g = {0: means[0]} | {s: along_feat(means[s], s) for s in (2, 1, 3)}
    g = [g[s] for s in range(NF)]
    z_block = pl.pallas_call(
        hidden_kernel, out_shape=jax.ShapeDtypeStruct((TILE, TILE), bf16),
        in_specs=[VM] * 9, out_specs=VM,
        scratch_shapes=[pltpu.VMEM((SHARE, 512), f32)],
        compiler_params=params(), cost_estimate=cost(2 * 96 * 768 * 1024, 2e6), name="hidden",
    )(*g, whole, side, other_side, near, far)

    ring = {0: z_block} | {s: first_axis(z_block, s) for s in (2, 1, 3)}
    z_four = jnp.stack([ring[s] for s in SHIFTS])
    z_rows = {0: z_four} | {t: second_axis(z_four, t) for t in (2, 1, 3)}
    z_rows = [z_rows[t] for t in SHIFTS]
    z_rows = dict(zip(SHIFTS, z_rows, strict=True))
    z_other = {t: swap(z_rows[t]) for t in SHIFTS}
    z_shape = pltpu.VMEM((NV * TILE, 256), bf16)
    early = ((0, 0), (0, 1), (2, 0), (1, 0), (3, 0))
    late = ((2, 1), (1, 1), (3, 1))
    z_all = pl.pallas_call(
        functools.partial(unpack_kernel, early), out_shape=z_shape,
        in_specs=[VM] * len(early), out_specs=VM,
        compiler_params=params(), cost_estimate=cost(1e5, 2e6), name="unpack",
    )(*((z_rows, z_other)[p][t] for t, p in early))
    part, _ = pl.pallas_call(
        functools.partial(scores_kernel, late),
        out_shape=[jax.ShapeDtypeStruct((160, ROWS), bf16), z_shape],
        in_specs=[VM] * (3 + len(late)), out_specs=[VM] * 2, input_output_aliases={2: 1},
        compiler_params=params(), cost_estimate=cost(2 * 384 * 4096 * 256, 5e6), name="scores",
    )(adj2, degree, z_all, *((z_rows, z_other)[p][t] for t, p in late))
    parts = {0: part} | {s: along_feat(part, s) for s in (2, 1, 3)}
    parts = [parts[s] for s in range(NF)]
    return pl.pallas_call(
        sum_kernel, out_shape=jax.ShapeDtypeStruct((CLS, ROWS), f32),
        in_specs=[VM] * 5, out_specs=VM,
        compiler_params=params(), cost_estimate=cost(3e5, 8e5), name="sum",
    )(*parts, jnp.pad(b_out, (0, 256 - CLS)).reshape(1, 256)).T


def solution(mesh):
    placed = (
        P("vert", "feat"),
        P("vert", None),
        P("vert", None),
        P("feat", None),
        P("feat"),
        P("feat", None),
        P(),
    )
    return jax.shard_map(
        local, mesh=mesh, in_specs=placed, out_specs=P("vert", None), check_vma=False
    )
```

```python
import functools

import jax
import jax.numpy as jnp
from jax import lax
from jax.experimental import pallas as pl
from jax.experimental.pallas import tpu as pltpu
from jax.sharding import PartitionSpec as P

TILE = 128
ROWS = 384
NV = 32
NF = 4
SHARE = ROWS // NF
CLS = 153
bf16 = jnp.bfloat16
f32 = jnp.float32
NT = (((1,), (1,)), ((), ()))
VM = pl.BlockSpec(memory_space=pltpu.VMEM)
SM = pl.BlockSpec(memory_space=pltpu.SMEM)
HB = pl.BlockSpec(memory_space=pltpu.HBM)
ANY = pl.BlockSpec(memory_space=pl.ANY)


def here():
    return lax.axis_index("vert").astype(jnp.int32), lax.axis_index("feat").astype(jnp.int32)


def source(me, s, t, c):
    spot = lax.div(me, 2)
    x, z = lax.div(spot, NF), lax.rem(spot, NF)
    x = lax.rem(x + NF - jnp.where(c == 0, s, t), NF)
    z = lax.rem(z + NF - jnp.where(c == 0, t, s), NF)
    return (x * NF + z) * 2 + c


SHIFTS = (0, 2, 1, 3)


def params(mib=16):
    return pltpu.CompilerParams(vmem_limit_bytes=mib * 2**20)


def cost(flops, nbytes):
    return pl.CostEstimate(flops=int(flops), bytes_accessed=int(nbytes), transcendentals=0)


def positions(move):
    pairs = []
    for x in range(4):
        for z in range(4):
            for c in range(2):
                xx, zz, cc = move(x, z, c)
                pairs.append(((x * 4 + z) * 2 + c, (xx % 4 * 4 + zz % 4) * 2 + cc % 2))
    return pairs


def first_axis(value, shift):
    return lax.ppermute(value, "vert", positions(lambda x, z, c: (x + shift * (1 - c), z + shift * c, c)))


def second_axis(value, shift):
    return lax.ppermute(value, "vert", positions(lambda x, z, c: (x + shift * c, z + shift * (1 - c), c)))


def swap(value):
    return lax.ppermute(value, "vert", positions(lambda x, z, c: (x, z, 1 - c)))


def along_feat(value, shift):
    return lax.ppermute(value, "feat", [(i, (i + shift) % NF) for i in range(NF)])


def both_sides(value):
    pairs = [(f * NV + v, (f + 1 - 2 * (v % 2)) % NF * NV + v) for v in range(NV) for f in range(NF)]
    return lax.ppermute(value, ("feat", "vert"), pairs)


CHUNK = 4 * ROWS
STEPS = NV * ROWS // CHUNK
SLOTS = 3
SPLIT = 3


def adjacency_kernel(part, mask, counts, *refs):
    if part == 0:
        w_in, w_out_t, b_in, adj, adj2, degree, whole, mine, slots, sems, mask_sm, one, w1, w2, b1, three = refs
        extra = [(w_in, w1), (w_out_t, w2), (b_in, b1)]
    else:
        adj, adj2, degree, slots, sems, mask_sm, one = refs[4:]
        extra = []
    me, feat = here()
    first, last = (0, SPLIT) if part == 0 else (SPLIT, STEPS)
    mask_copy = pltpu.make_async_copy(mask, mask_sm, one)
    mask_copy.start()
    source_row = lax.broadcasted_iota(jnp.int32, (ROWS, TILE), 0)
    target = lax.broadcasted_iota(jnp.int32, (ROWS, TILE), 1)
    chosen = (source_row == target + feat * SHARE) & (target < SHARE)
    pick = (chosen | (target == SHARE)).astype(f32).astype(bf16)
    inside = lax.broadcasted_iota(jnp.int32, (TILE, TILE), 1) < SHARE

    def fetch(step, slot):
        start = pl.multiple_of(step * CHUNK, CHUNK)
        return pltpu.make_async_copy(counts.at[:, pl.ds(start, CHUNK)], slots.at[slot], sems.at[slot])

    for i in range(SLOTS - 1):
        fetch(first + i, i).start()
    extra = [pltpu.make_async_copy(a, b, three.at[i]) for i, (a, b) in enumerate(extra)]
    for copy in extra:
        copy.start()
    if part == 0:
        degree[...] = jnp.zeros_like(degree)
    mask_copy.wait()

    @pl.loop(first, last)
    def _(step):
        slot = lax.rem(step - first, SLOTS)

        @pl.when(step + SLOTS - 1 < last)
        def _():
            fetch(step + SLOTS - 1, lax.rem(step - first + SLOTS - 1, SLOTS)).start()

        fetch(step, slot).wait()
        for j in range(CHUNK // ROWS):
            base = pl.multiple_of(step * CHUNK + j * ROWS, ROWS)
            place = pl.multiple_of((step * (CHUNK // ROWS) + j) * TILE, TILE)
            for i in range(ROWS // TILE):
                rows = slice(i * TILE, (i + 1) * TILE)
                strip = []
                for k in range(ROWS // TILE):
                    stored = mask_sm[i, (step * (CHUNK // ROWS) + j) * (ROWS // TILE) + k].astype(f32)
                    tile = slots[slot, rows, j * ROWS + k * TILE : j * ROWS + (k + 1) * TILE]
                    strip.append((tile.astype(f32) * stored).astype(bf16))
                strip = jnp.concatenate(strip, axis=1)
                adj[rows, pl.ds(base, ROWS)] = strip
                part = jnp.dot(strip, pick, preferred_element_type=f32)
                degree[rows, :] += part
                adj2[rows, pl.ds(place, TILE)] = jnp.where(inside, part, 0.0).astype(bf16)

    for copy in extra:
        copy.wait()
    if part == 0:
        pack(w1, w2, b1, whole, mine)
        return
    place = pl.ds(pl.multiple_of(me * TILE, TILE), TILE)
    adj2[:, place] = (adj2[:, place].astype(f32) + chosen.astype(f32)).astype(bf16)
    row = lax.broadcasted_iota(jnp.int32, (ROWS, ROWS), 0)
    col = lax.broadcasted_iota(jnp.int32, (ROWS, ROWS), 1)
    place = pl.ds(pl.multiple_of(me * ROWS, ROWS), ROWS)
    adj[:, place] = (adj[:, place].astype(f32) + (row == col).astype(f32)).astype(bf16)
    degree[...] = jnp.broadcast_to(1.0 / (degree[:, SHARE : SHARE + 1] + 1.0), degree.shape)


ADJACENCY = [
    pltpu.VMEM((ROWS, NV * ROWS), bf16),
    pltpu.VMEM((ROWS, NV * TILE), bf16),
    pltpu.VMEM((ROWS, TILE), f32),
]
ADJACENCY_SCRATCH = [
    pltpu.VMEM((SLOTS, ROWS, CHUNK), jnp.int32),
    pltpu.SemaphoreType.DMA((SLOTS,)),
    pltpu.SMEM((ROWS // TILE, NV * ROWS // TILE), jnp.int32),
    pltpu.SemaphoreType.DMA(()),
]


def first_half(tile_mask, counts, w_in, w_out_t, b_in):
    return pl.pallas_call(
        functools.partial(adjacency_kernel, 0),
        in_specs=[HB] * 5,
        out_specs=[VM] * 5,
        out_shape=ADJACENCY + [
            jax.ShapeDtypeStruct((2, 256, 512), bf16),
            jax.ShapeDtypeStruct((256, 512), bf16),
        ],
        scratch_shapes=ADJACENCY_SCRATCH + [
            pltpu.VMEM((192, 1024), bf16),
            pltpu.VMEM((CLS, 256), bf16),
            pltpu.VMEM((1, 256), f32),
            pltpu.SemaphoreType.DMA((3,)),
        ],
        compiler_params=params(24),
        cost_estimate=cost(1.2e9, 16e6),
        name="adjacency_first",
    )(tile_mask, counts, w_in, w_out_t, b_in)


def second_half(tile_mask, counts, adj, adj2, degree, after):
    return pl.pallas_call(
        functools.partial(adjacency_kernel, 1),
        in_specs=[HB] * 2 + [VM] * 3 + [ANY],
        out_specs=[VM] * 3,
        out_shape=ADJACENCY,
        input_output_aliases={2: 0, 3: 1, 4: 2},
        scratch_shapes=ADJACENCY_SCRATCH,
        compiler_params=params(24),
        cost_estimate=cost(1.2e9, 16e6),
        name="adjacency_second",
    )(tile_mask, counts, adj, adj2, degree, after)


def pack(w_in, w_out_t, b_in, whole, mine):
    zero = jnp.zeros((192 - CLS, TILE), f32)
    for half in range(2):
        lanes = slice(TILE * half, TILE * (half + 1))
        for k in range(NF):
            whole[half, 0:192, k * TILE : (k + 1) * TILE] = w_in[:, 256 * k + TILE * half : 256 * k + TILE * (half + 1)]
        w = jnp.concatenate([w_out_t[:, lanes].astype(f32), zero], axis=0)
        for k in range(NF):
            whole[half, 192:240, k * TILE : (k + 1) * TILE] = w[48 * k : 48 * (k + 1)].astype(bf16)
        b = jnp.broadcast_to(b_in[:, lanes], (16, TILE))
        hi = b.astype(bf16).astype(f32)
        mid = (b - hi).astype(bf16).astype(f32)
        low = b - hi - mid
        row = lax.broadcasted_iota(jnp.int32, (16, TILE), 0)
        b = jnp.where(row == 0, hi, jnp.where(row == 1, mid, jnp.where(row == 2, low, 0.0)))
        whole[half, 240:256, 0:TILE] = b.astype(bf16)
        whole[half, 240:256, TILE:] = jnp.zeros((16, 512 - TILE), bf16)
    mine[...] = whole[lax.rem(here()[0], 2)]


def stack_kernel(a, b, c, d, after, out):
    for i, part in enumerate((a, b, c, d)):
        out[i] = part[...]


def add_blocks(kinds, adj, total, pieces):
    me, _ = here()
    for (shift, p), piece in zip(kinds, pieces, strict=True):
        core = lax.rem(me + p, 2)
        for b in range(NF):
            src = source(me, SHIFTS[b], shift, core)
            src = pl.multiple_of(src * ROWS, ROWS)
            total = total + lax.dot_general(adj[:, pl.ds(src, ROWS)], piece[b], NT, preferred_element_type=f32)
    return total


def product_first(kinds, adj, *refs):
    refs[-1][...] = add_blocks(kinds, adj, jnp.zeros(refs[-1].shape, f32), refs[: len(kinds)])


def product_next(kinds, adj, before, *refs):
    refs[-1][...] = add_blocks(kinds, adj, before[...], refs[: len(kinds)])


def product_last(kinds, adj, before, degree, *refs):
    pieces, outs, mean = refs[: len(kinds)], refs[-5:-1], refs[-1]
    feat = here()[1]
    total = add_blocks(kinds, adj, before[...], pieces)
    mean[...] = total * degree[:, :1]
    for s in range(NF):
        q = lax.rem(feat + s, NF)
        outs[s][...] = mean[pl.ds(pl.multiple_of(q * SHARE, SHARE), SHARE), :].astype(bf16)


def blocks_cost(pieces):
    n = sum(p.shape[0] for p in pieces)
    return cost(2 * 384 * 384 * 256 * n, n * 450e3)


def hidden_kernel(g0, g1, g2, g3, own, side, other_side, near, far, z_out, hid):
    me, feat = here()
    core = lax.rem(me, 2)
    even = core == 0
    ga = jnp.where(even, g1[...].astype(f32), g3[...].astype(f32)).astype(bf16)
    gb = jnp.where(even, g3[...].astype(f32), g1[...].astype(f32)).astype(bf16)
    down, up = lax.rem(feat + NF - 1, NF), lax.rem(feat + 1, NF)
    across = lax.rem(feat + 2, NF)
    total = jnp.zeros((SHARE, 192), f32)
    for half, opposite in ((core, near), (1 - core, far)):
        parts = (
            (g0[...], own.at[half], feat),
            (ga, side.at[half], jnp.where(even, down, up)),
            (gb, other_side.at[half], jnp.where(even, up, down)),
            (g2[...], opposite, across),
        )
        pre = jnp.zeros((SHARE, 512), f32)
        for g, part, _ in parts:
            pre = pre + jnp.dot(g, part[0:192, :], preferred_element_type=f32)
        hid[...] = pre
        for _, part, owner in parts:
            lanes = pl.ds(pl.multiple_of(owner * TILE, TILE), TILE)
            b = part[240:256, 0:TILE].astype(f32)
            bias = b[0:1] + b[1:2] + b[2:3]
            unit = jnp.maximum(hid[:, lanes] + bias, 0.0).astype(bf16)
            w = part[192:240, :]
            w = jnp.concatenate([w[:, k * TILE : (k + 1) * TILE] for k in range(NF)], axis=0)
            total = total + lax.dot_general(unit, w, NT, preferred_element_type=f32)
    z_out[0:SHARE, :] = total[:, :TILE].astype(bf16)
    tail = total[:, TILE : TILE + 32]
    packed = jnp.concatenate([tail[0:32], tail[32:64], tail[64:96], jnp.zeros((32, 32), f32)], axis=1)
    z_out[SHARE:, :] = packed.astype(bf16)


def unpack(kinds, pieces, z_all):
    me, _ = here()
    for (shift, p), piece in zip(kinds, pieces, strict=True):
        for b in range(NF):
            src = source(me, SHIFTS[b], shift, lax.rem(me + p, 2))
            src = pl.multiple_of(src * TILE, TILE)
            z_all[pl.ds(src, TILE), :TILE] = piece[b]
            tail = piece[b, SHARE:, :].astype(f32)
            tail = jnp.concatenate([tail[:, 0:32], tail[:, 32:64], tail[:, 64:96], jnp.zeros((32, 32), f32)], axis=0)
            tail = jnp.concatenate([tail, jnp.zeros((TILE, 96), f32)], axis=1)
            z_all[pl.ds(src, TILE), TILE:] = tail.astype(bf16)


def unpack_kernel(kinds, *refs):
    unpack(kinds, refs[: len(kinds)], refs[-1])


def scores_kernel(kinds, adj2, inverse, before, *refs):
    out, z_all = refs[-2], refs[-1]
    unpack(kinds, refs[: len(kinds)], z_all)
    part = jnp.dot(adj2[...], z_all[...], preferred_element_type=f32) * inverse[:, :1]
    out[...] = part.T[0:160].astype(bf16)


def sum_kernel(p0, p2, p1, p3, b_out, out):
    total = (p0[...].astype(f32) + p2[...].astype(f32)) + (p1[...].astype(f32) + p3[...].astype(f32))
    bias = jnp.broadcast_to(b_out[...], (TILE, 256)).T[:, 0:1]
    out[...] = total[0:CLS] + bias[0:CLS]


def local(features, counts, tile_mask, w_in, b_in, w_out, b_out):
    tile_mask, counts, *weights = (
        pltpu.with_memory_space_constraint(a, pltpu.HBM)
        for a in (tile_mask, counts, w_in, w_out.T, b_in.reshape(1, 256))
    )
    *adjacency, whole, mine_half = first_half(tile_mask, counts, *weights)
    near = along_feat(mine_half, 2)

    mine = features.T
    ring = [first_axis(mine, s) for s in (2, 1, 3)]
    four = pl.pallas_call(
        stack_kernel, out_shape=jax.ShapeDtypeStruct((NF, 192, ROWS), bf16),
        in_specs=[VM] * 4 + [ANY], out_specs=VM,
        compiler_params=params(), cost_estimate=cost(1e5, 1.2e6), name="stack",
    )(mine, *ring, mine_half)
    rows = {t: second_axis(four, t) for t in (2, 1, 3)}

    other_four = swap(four)
    side = both_sides(whole)
    adj, adj2, degree = second_half(tile_mask, counts, *adjacency, other_four)

    total_shape = jax.ShapeDtypeStruct((ROWS, 192), f32)
    def product(kernel, kinds, pieces, *extra, after=(), name):
        return pl.pallas_call(
            functools.partial(kernel, kinds), out_shape=total_shape,
            in_specs=[VM] * (1 + len(extra) + len(pieces)) + [ANY] * len(after), out_specs=VM,
            compiler_params=params(), cost_estimate=blocks_cost(pieces), name=name,
        )(adj, *extra, *pieces, *after)

    total = product(product_first, ((0, 0), (0, 1)), [four, other_four], after=(side,), name="product_first")
    for t in (1, 2, 3):
        rows[t] = lax.optimization_barrier((total, rows[t]))[1]
    total = product(product_next, ((1, 0), (3, 0)), [rows[1], rows[3]], total, after=(near,), name="product_next")
    rows[2] = lax.optimization_barrier((total, rows[2]))[1]
    other_side = swap(lax.optimization_barrier((side, total))[0])
    far = swap(lax.optimization_barrier((near, total))[0])
    across = swap(rows[2])
    pieces = [swap(rows[1]), swap(rows[3]), rows[2]]
    total = product(product_next, ((1, 1), (3, 1), (2, 0)), pieces, total, name="product_more")
    pieces = [across]
    means = pl.pallas_call(
        functools.partial(product_last, ((2, 1),)), out_shape=[jax.ShapeDtypeStruct((SHARE, 192), bf16)] * NF,
        in_specs=[VM] * 4 + [ANY] * 2, out_specs=[VM] * NF,
        scratch_shapes=[pltpu.VMEM((ROWS, 192), f32)],
        compiler_params=params(), cost_estimate=blocks_cost(pieces), name="product_last",
    )(adj, total, degree, *pieces, other_side, far)

    g = {0: means[0]} | {s: along_feat(means[s], s) for s in (2, 1, 3)}
    g = [g[s] for s in range(NF)]
    z_block = pl.pallas_call(
        hidden_kernel, out_shape=jax.ShapeDtypeStruct((TILE, TILE), bf16),
        in_specs=[VM] * 9, out_specs=VM,
        scratch_shapes=[pltpu.VMEM((SHARE, 512), f32)],
        compiler_params=params(), cost_estimate=cost(2 * 96 * 768 * 1024, 2e6), name="hidden",
    )(*g, whole, side, other_side, near, far)

    ring = {0: z_block} | {s: first_axis(z_block, s) for s in (2, 1, 3)}
    z_four = jnp.stack([ring[s] for s in SHIFTS])
    z_rows = {0: z_four} | {t: second_axis(z_four, t) for t in (2, 1, 3)}
    z_rows = [z_rows[t] for t in SHIFTS]
    z_rows = dict(zip(SHIFTS, z_rows, strict=True))
    z_other = {t: swap(z_rows[t]) for t in SHIFTS}
    z_shape = pltpu.VMEM((NV * TILE, 256), bf16)
    early = ((0, 0), (0, 1), (2, 0), (1, 0), (3, 0))
    late = ((2, 1), (1, 1), (3, 1))
    z_all = pl.pallas_call(
        functools.partial(unpack_kernel, early), out_shape=z_shape,
        in_specs=[VM] * len(early), out_specs=VM,
        compiler_params=params(), cost_estimate=cost(1e5, 2e6), name="unpack",
    )(*((z_rows, z_other)[p][t] for t, p in early))
    part, _ = pl.pallas_call(
        functools.partial(scores_kernel, late),
        out_shape=[jax.ShapeDtypeStruct((160, ROWS), bf16), z_shape],
        in_specs=[VM] * (3 + len(late)), out_specs=[VM] * 2, input_output_aliases={2: 1},
        compiler_params=params(), cost_estimate=cost(2 * 384 * 4096 * 256, 5e6), name="scores",
    )(adj2, degree, z_all, *((z_rows, z_other)[p][t] for t, p in late))
    parts = {0: part} | {s: along_feat(part, s) for s in (2, 1, 3)}
    parts = [parts[s] for s in SHIFTS]
    return pl.pallas_call(
        sum_kernel, out_shape=jax.ShapeDtypeStruct((CLS, ROWS), f32),
        in_specs=[VM] * 5, out_specs=VM,
        compiler_params=params(), cost_estimate=cost(3e5, 8e5), name="sum",
    )(*parts, jnp.pad(b_out, (0, 256 - CLS)).reshape(1, 256)).T


def solution(mesh):
    placed = (
        P("vert", "feat"),
        P("vert", None),
        P("vert", None),
        P("feat", None),
        P("feat"),
        P("feat", None),
        P(),
    )
    return jax.shard_map(
        local, mesh=mesh, in_specs=placed, out_specs=P("vert", None), check_vma=False
    )
```
